512 devices in a mesh: freq: 8 (over x, core), tile: 64 (over z, y).
Axes of the slice: x: 4, y: 4, z: 16, core: 2. Of those that a mesh axis runs over, the one named last changes fastest.
Arguments:
- model_start: float32 [8, 16384, 128], P('freq', 'tile'), may hold values from -6 to 6
- data: bfloat16 [8, 16384, 128], P('freq', 'tile'), may hold values from -6 to 6
- col_factors: bfloat16 [8, 512, 2, 112, 256], P('freq', 'tile'), may hold values from -0.375 to 0.375
- row_factors: bfloat16 [8, 512, 2, 112, 256], P('freq', 'tile'), may hold values from -0.1875 to 0.1875
- ranks: int32 [8, 64, 8], P('freq'), may hold values from 16 to 112
- gate_window: int32 [64, 2], replicated, may hold values from 0 to 2047, as said below
- step_sizes: float32 [8], P('freq'), may hold values from 0.2 to 0.6
Outputs:
- model_final: float32 [8, 16384, 128], P('freq', 'tile')
The draws below stay inside these ranges and needn't reach their ends.
Inputs may be any that keep to these rules, and one draw needn't show every extreme that they name: `gate_window`: each row is (start, end) with 256 <= end - start <= 1024.
All inputs are finite; a program needn't handle non-finite values.
Results may differ from the reference program's by a relative error of at most 0.0085.
Values may be sent and summed in bfloat16 or wider, within the bound.
No kernel may reach another device: no remote copies, remote signals or barrier semaphores. Data moves between devices by JAX's collectives and lax.ppermute only.
A program may use at most 64 MiB of HBM per device.

```python
import math
import jax
import jax.numpy as jnp
from jax import lax

B = 256
RMAX = 112
RMIN = 16
TPD = 8
NV = 64
NT = 2048
ITERS = 2
FREQS = 8
NS = 16384
NR = 16384
SLOTS = 512
N_TILE = 64


def draw_gate_window(key, part):
    first, second = jax.random.split(jax.random.fold_in(key, 23), 2)
    opening = jax.random.randint(first, (NV,), 0, NT // 2, dtype=jnp.int32)
    length = jax.random.randint(second, (NV,), NT // 8, NT // 2 + 1, dtype=jnp.int32)
    return jnp.stack([opening, opening + length], axis=-1).astype(jnp.int32)


def touch_ends(entries, own_key, smallest, largest):
    longest = entries.shape.index(max(entries.shape))
    spots = []
    for shift in (0, 1):
        where = [jax.random.randint(jax.random.fold_in(own_key, axis), (), 0, length) for axis, length in enumerate(entries.shape)]
        where[longest] = (where[longest] + shift) % entries.shape[longest]
        spots.append(tuple(where))
    return entries.at[spots[0]].set(smallest).at[spots[1]].set(largest)


def block_scale(rng, dims, shards, smallest, top_value):
    gain = 1.0
    for position, parts in shards:
        heights = jax.random.uniform(jax.random.fold_in(jax.random.fold_in(rng, 6), position), (parts,), jnp.float32, smallest / len(shards), top_value / len(shards))
        gain = gain * jnp.repeat(jnp.exp(heights), dims[position] // parts).reshape((-1,) + (1,) * (len(dims) - 1 - position))
    return gain


def normal_values(stream_key, extent, deviation, reach, cuts=(), kind=jnp.bfloat16):
    drawn = jax.random.normal(stream_key, extent, jnp.float32) * deviation
    if len(cuts) > 0:
        drawn = block_scale(stream_key, extent, cuts, -0.22, 0.18) * drawn
    return jnp.clip(drawn, min=-reach, max=reach).astype(kind)


def setup_inputs(seed: int = 0) -> dict:
    keys = jax.random.split(jax.random.key(seed), 8)
    return {
        "model_start": normal_values(keys[0], (FREQS, NS, 2 * NV), 1.0, 6.0, ((0, 8), (1, 64)), jnp.float32),
        "data": normal_values(keys[1], (FREQS, NR, 2 * NV), 1.0, 6.0, ((0, 8), (1, 64))),
        "col_factors": normal_values(keys[2], (FREQS, SLOTS, 2, RMAX, B), B ** -0.5, 0.375, ((0, 8), (1, 64))),
        "row_factors": normal_values(keys[3], (FREQS, SLOTS, 2, RMAX, B), (TPD * RMAX) ** -0.5, 0.1875, ((0, 8), (1, 64))),
        "ranks": touch_ends(jax.random.randint(keys[4], (FREQS, N_TILE, TPD), RMIN, RMAX + 1), jax.random.fold_in(keys[4], 1), RMIN, RMAX).astype(jnp.int32),
        "gate_window": draw_gate_window(jax.random.fold_in(keys[7], 71), 0),
        "step_sizes": jnp.clip(jnp.exp(math.log(0.6) - 1.0986123 * jax.random.uniform(keys[6], (FREQS,), jnp.float32) ** block_scale(keys[6], (FREQS,), ((0, 8),), -0.2, 0.2)), 0.2, 0.6),
    }


def rotate(z):
    half = z.shape[-1] // 2
    return jnp.concatenate([-z[..., half:], z[..., :half]], axis=-1)


def gate_matrix(window, count):
    start = window[:, 0].astype(jnp.float32)
    span = (window[:, 1] - window[:, 0]).astype(jnp.float32)
    freqs = jnp.arange(count, dtype=jnp.float32)
    delta = freqs[:, None] - freqs[None, :]
    theta = 2.0 * math.pi * delta / NT
    safe = jnp.where(delta == 0.0, 1.0, jnp.sin(theta / 2.0))
    magnitude = jnp.where((delta == 0.0)[:, :, None], span[None, None, :] / NT,
                          jnp.sin(theta[:, :, None] * span[None, None, :] / 2.0) / (NT * safe[:, :, None]))
    phase = theta[:, :, None] * (start[None, None, :] + (span[None, None, :] - 1.0) / 2.0)
    return magnitude * jnp.cos(phase), magnitude * jnp.sin(phase)


def one_step(inputs):
    model, data, col_factors, row_factors, ranks, stepping = inputs
    f32 = jnp.float32
    vfac = col_factors.reshape(N_TILE, TPD, 2, RMAX, B).astype(f32)
    ufac = row_factors.reshape(N_TILE, TPD, 2, RMAX, B).astype(f32)
    slots = jnp.arange(TPD, dtype=jnp.int32)[None, :]
    offsets = slots - TPD // 2
    blocks = jnp.arange(N_TILE, dtype=jnp.int32)[:, None]
    target = blocks + offsets
    target_ok = (target >= 0) & (target < N_TILE)
    anchor = blocks - offsets
    anchor_ok = (anchor >= 0) & (anchor < N_TILE)
    target_c = jnp.clip(target, 0, N_TILE - 1).astype(jnp.int32)
    anchor_c = jnp.clip(anchor, 0, N_TILE - 1).astype(jnp.int32)
    levels = jnp.arange(RMAX, dtype=jnp.int32)
    xb = model.reshape(N_TILE, B, 2 * NV).astype(jnp.bfloat16).astype(f32)
    coef = jnp.einsum('csrb,cbv->csrv', vfac[:, :, 0], xb) + jnp.einsum('csrb,cbv->csrv', vfac[:, :, 1], rotate(xb))
    col_mask = (levels[None, None, :] < ranks[:, :, None]).astype(f32)
    coef = (coef * col_mask[..., None]).astype(jnp.bfloat16).astype(f32)
    received = coef[anchor_c, slots] * anchor_ok.astype(f32)[..., None, None]
    image = jnp.einsum('rskb,rskv->rbv', ufac[:, :, 0], received) + jnp.einsum('rskb,rskv->rbv', ufac[:, :, 1], rotate(received))
    resid = (image - data.reshape(N_TILE, B, 2 * NV).astype(f32)).astype(jnp.bfloat16).astype(f32)
    row_rank = jnp.where(anchor_ok, ranks[anchor_c, slots], 0)
    row_mask = (levels[None, None, :] < row_rank[:, :, None]).astype(f32)
    return_trip = jnp.einsum('rskb,rbv->rskv', ufac[:, :, 0], resid) - jnp.einsum('rskb,rbv->rskv', ufac[:, :, 1], rotate(resid))
    return_trip = (return_trip * row_mask[..., None]).astype(jnp.bfloat16).astype(f32)
    returned = return_trip[target_c, slots] * target_ok.astype(f32)[..., None, None]
    grad = jnp.einsum('csrb,csrv->cbv', vfac[:, :, 0], returned) - jnp.einsum('csrb,csrv->cbv', vfac[:, :, 1], rotate(returned))
    return model - stepping * grad.reshape(N_TILE * B, 2 * NV)


def reference(model_start, data, col_factors, row_factors, ranks, gate_window, step_sizes):
    count = model_start.shape[0]
    gate_re, gate_im = gate_matrix(gate_window, count)
    model = model_start
    for step in range(ITERS):
        moved = lax.map(one_step, (model, data, col_factors, row_factors, ranks, step_sizes))
        part_re = moved[..., :NV]
        part_im = moved[..., NV:]
        hp = lax.Precision.HIGHEST
        new_re = jnp.einsum('fgv,gnv->fnv', gate_re, part_re, precision=hp) - jnp.einsum('fgv,gnv->fnv', gate_im, part_im, precision=hp)
        new_im = jnp.einsum('fgv,gnv->fnv', gate_re, part_im, precision=hp) + jnp.einsum('fgv,gnv->fnv', gate_im, part_re, precision=hp)
        model = jnp.concatenate([new_re, new_im], axis=-1)
    return model
```

```python
import math

import jax
import jax.numpy as jnp
from jax import lax
from jax.sharding import PartitionSpec as P

NT = 2048
ITERS = 2
WIDE = 4


def rotate(z):
    half = z.shape[-1] // 2
    return jnp.concatenate([-z[..., half:], z[..., :half]], axis=-1)


def gate_matrix(window, count):
    start = window[:, 0].astype(jnp.float32)
    span = (window[:, 1] - window[:, 0]).astype(jnp.float32)
    freqs = jnp.arange(count, dtype=jnp.float32)
    delta = freqs[:, None] - freqs[None, :]
    theta = 2.0 * math.pi * delta / NT
    safe = jnp.where(delta == 0.0, 1.0, jnp.sin(theta / 2.0))
    magnitude = jnp.where(
        (delta == 0.0)[:, :, None],
        span[None, None, :] / NT,
        jnp.sin(theta[:, :, None] * span[None, None, :] / 2.0) / (NT * safe[:, :, None]),
    )
    phase = theta[:, :, None] * (start[None, None, :] + (span[None, None, :] - 1.0) / 2.0)
    return (magnitude * jnp.cos(phase), magnitude * jnp.sin(phase))


def left_dot(factor, values):
    return lax.dot_general(
        factor, values, (((0,), (0,)), ((), ())), preferred_element_type=jnp.float32
    )


def complex_mix(coeff_re, coeff_im, values):
    values = values.astype(jnp.float32)
    width = values.shape[-1] // 2
    vals_re = values[..., :width]
    vals_im = values[..., width:]
    out_re = jnp.sum(coeff_re[:, None, :] * vals_re - coeff_im[:, None, :] * vals_im, axis=0)
    out_im = jnp.sum(coeff_re[:, None, :] * vals_im + coeff_im[:, None, :] * vals_re, axis=0)
    return jnp.concatenate([out_re, out_im], axis=-1)


def on_device(model_start, data, col_factors, row_factors, ranks, gate_window, step_sizes):
    ntile = lax.axis_size("tile")
    nfreq = lax.axis_size("freq")
    myself = lax.axis_index("tile")
    my_freq = lax.axis_index("freq")
    slots = ranks.shape[2]
    levels = col_factors.shape[3]
    half = slots // 2
    rows_z = ntile // WIDE
    col = myself % WIDE
    odd = (myself // WIDE) % 2 == 1
    groups = [[slots * k + i for i in range(slots)] for k in range(ntile // slots)]
    swaps = [
        (z * WIDE + y, (z + 1 if z % 2 else z - 1) * WIDE + y)
        for z in range(1, rows_z - 1)
        for y in range(WIDE)
    ]

    def swap(value):
        return lax.ppermute(value, "tile", swaps)

    def spread(own, forwarded):
        send = jnp.stack([own, jnp.concatenate([forwarded, forwarded])], axis=1)
        got = lax.all_to_all(send, "tile", 0, 0, tiled=True, axis_index_groups=groups)
        return got[:, 0], got[:, 1]

    def by_parity(same, cross):
        return jnp.where(
            odd, jnp.concatenate([cross, same]), jnp.concatenate([same, cross])
        )

    def cross_half(pieces):
        return jnp.where(odd, pieces[:half], pieces[half:])

    def same_half(pieces):
        return jnp.where(odd, pieces[half:], pieces[:half])

    def in_order(table, start_same, start_cross):
        twice = jnp.concatenate([table, table])
        same = lax.dynamic_slice_in_dim(table, start_same, half, 0)
        cross = lax.dynamic_slice_in_dim(twice, start_cross, half, 0)
        return by_parity(same, cross)

    others = jnp.arange(half, dtype=jnp.int32)
    direct_in = jnp.where(odd, col < others, col >= others)
    direct_out = jnp.where(odd, others >= col, others < col)
    none = jnp.zeros((half,), bool)
    relay_in = by_parity(none, jnp.logical_not(direct_in))[:, None, None]
    relay_out = by_parity(none, jnp.logical_not(direct_out))[:, None, None]

    v = in_order(col_factors[0], 4 - col, 8 - col)
    u = in_order(row_factors[0][::-1], 3 - col, 7 - col)
    v_real, v_imag = (v[:, i].reshape(slots * levels, -1) for i in range(2))
    u_real, u_imag = (u[:, i].reshape(slots * levels, -1) for i in range(2))

    rank_table = ranks[0]
    my_ranks = lax.dynamic_index_in_dim(rank_table, myself, 0, keepdims=False)
    anchors = myself - (jnp.arange(slots, dtype=jnp.int32) - half)
    holder = jnp.arange(ntile, dtype=jnp.int32)[:, None] == anchors[None, :]
    row_ranks = jnp.sum(jnp.where(holder, rank_table, 0), axis=0)
    level_ids = jnp.arange(levels, dtype=jnp.int32)
    col_mask = (level_ids[None, :] < in_order(my_ranks, 4 - col, 8 - col)[:, None])[..., None]
    row_mask = (
        level_ids[None, :] < in_order(row_ranks[::-1], 3 - col, 7 - col)[:, None]
    )[..., None]

    gate_re, gate_im = gate_matrix(gate_window, nfreq)
    row_re = lax.dynamic_index_in_dim(gate_re, my_freq, 0, keepdims=False)
    row_im = lax.dynamic_index_in_dim(gate_im, my_freq, 0, keepdims=False)
    stepping = step_sizes[0]
    model = model_start[0]
    observed = data[0].astype(jnp.float32)
    width = model.shape[-1]
    for step in range(ITERS):
        model_bf = model.astype(jnp.bfloat16)
        coef = jnp.dot(v_real, model_bf, preferred_element_type=jnp.float32) + jnp.dot(
            v_imag, rotate(model_bf), preferred_element_type=jnp.float32
        )
        coef = jnp.where(col_mask, coef.reshape(slots, levels, width), 0.0).astype(jnp.bfloat16)
        direct, relayed = spread(coef, swap(cross_half(coef)))
        relayed = same_half(relayed)
        placed = jnp.where(relay_in, jnp.concatenate([relayed, relayed]), direct)
        placed = placed.reshape(slots * levels, width)
        image = left_dot(u_real, placed) + left_dot(u_imag, rotate(placed))
        resid = (image - observed).astype(jnp.bfloat16)
        back = jnp.dot(u_real, resid, preferred_element_type=jnp.float32) - jnp.dot(
            u_imag, rotate(resid), preferred_element_type=jnp.float32
        )
        back = jnp.where(row_mask, back.reshape(slots, levels, width), 0.0).astype(jnp.bfloat16)
        direct, relayed = spread(back, cross_half(back))
        relayed = swap(same_half(relayed))
        landed = jnp.where(relay_out, jnp.concatenate([relayed, relayed]), direct)
        landed = landed.reshape(slots * levels, width)
        grad = left_dot(v_real, landed) - left_dot(v_imag, rotate(landed))
        updated = (model - stepping * grad).astype(jnp.bfloat16)
        everyone = lax.all_gather(updated, "freq", axis=0, tiled=False)
        model = complex_mix(row_re, row_im, everyone)
    return model[None]


def solution(mesh):
    return jax.shard_map(
        on_device,
        mesh=mesh,
        in_specs=(
            P("freq", "tile", None),
            P("freq", "tile", None),
            P("freq", "tile", None, None, None),
            P("freq", "tile", None, None, None),
            P("freq", None, None),
            P(),
            P("freq"),
        ),
        out_specs=P("freq", "tile", None),
        check_vma=False,
    )
```

```python
import math

import jax
import jax.numpy as jnp
from jax import lax
from jax.sharding import PartitionSpec as P

NT = 2048
ITERS = 2
WIDE = 4


def rotate(z):
    half = z.shape[-1] // 2
    return jnp.concatenate([-z[..., half:], z[..., :half]], axis=-1)


def gate_matrix(window, count):
    start = window[:, 0].astype(jnp.float32)
    span = (window[:, 1] - window[:, 0]).astype(jnp.float32)
    freqs = jnp.arange(count, dtype=jnp.float32)
    delta = freqs[:, None] - freqs[None, :]
    theta = 2.0 * math.pi * delta / NT
    safe = jnp.where(delta == 0.0, 1.0, jnp.sin(theta / 2.0))
    magnitude = jnp.where(
        (delta == 0.0)[:, :, None],
        span[None, None, :] / NT,
        jnp.sin(theta[:, :, None] * span[None, None, :] / 2.0) / (NT * safe[:, :, None]),
    )
    phase = theta[:, :, None] * (start[None, None, :] + (span[None, None, :] - 1.0) / 2.0)
    return (magnitude * jnp.cos(phase), magnitude * jnp.sin(phase))


def left_dot(factor, values):
    return lax.dot_general(
        factor, values, (((0,), (0,)), ((), ())), preferred_element_type=jnp.float32
    )


def complex_mix(coeff_re, coeff_im, values):
    width = values.shape[-1] // 2
    vals_re = values[..., :width]
    vals_im = values[..., width:]
    g_re = coeff_re[:, :, None, :]
    g_im = coeff_im[:, :, None, :]
    out_re = jnp.sum(g_re * vals_re - g_im * vals_im, axis=1)
    out_im = jnp.sum(g_re * vals_im + g_im * vals_re, axis=1)
    return jnp.concatenate([out_re, out_im], axis=-1)


def on_device(model_start, data, col_factors, row_factors, ranks, gate_window, step_sizes):
    ntile = lax.axis_size("tile")
    nfreq = lax.axis_size("freq")
    myself = lax.axis_index("tile")
    my_freq = lax.axis_index("freq")
    slots = ranks.shape[2]
    levels = col_factors.shape[3]
    half = slots // 2
    rows_z = ntile // WIDE
    col = myself % WIDE
    odd = (myself // WIDE) % 2 == 1
    groups = [[slots * k + i for i in range(slots)] for k in range(ntile // slots)]
    swaps = [
        (z * WIDE + y, (z + 1 if z % 2 else z - 1) * WIDE + y)
        for z in range(1, rows_z - 1)
        for y in range(WIDE)
    ]

    half_freq = [
        [
            f * ntile + (z % rows_z) * WIDE + y
            for f in range(nfreq)
            for z in (2 * k - 1, 2 * k)
        ]
        for k in range(rows_z // 2)
        for y in range(WIDE)
    ]

    def swap(value):
        return lax.ppermute(value, "tile", swaps)

    def spread(own, relayed):
        send = jnp.stack([own, jnp.concatenate([relayed, relayed])], axis=1)
        got = lax.all_to_all(send, "tile", 0, 0, tiled=True, axis_index_groups=groups)
        return got[:, 0], same_half(got[:, 1])

    def among_pair(pieces):
        flat = pieces.reshape(2 * nfreq, -1, pieces.shape[-1])
        got = lax.all_to_all(
            flat, ("freq", "tile"), 0, 0, tiled=True, axis_index_groups=half_freq
        )
        return got.reshape(pieces.shape)

    def by_parity(same, cross):
        return jnp.where(
            odd, jnp.concatenate([cross, same]), jnp.concatenate([same, cross])
        )

    def cross_half(pieces):
        return jnp.where(odd, pieces[:half], pieces[half:])

    def same_half(pieces):
        return jnp.where(odd, pieces[half:], pieces[:half])

    def in_order(table, start_same, start_cross):
        twice = jnp.concatenate([table, table])
        same = lax.dynamic_slice_in_dim(table, start_same, half, 0)
        cross = lax.dynamic_slice_in_dim(twice, start_cross, half, 0)
        return by_parity(same, cross)

    others = jnp.arange(half, dtype=jnp.int32)
    direct_in = jnp.where(odd, col < others, col >= others)
    direct_out = jnp.where(odd, others >= col, others < col)
    none = jnp.zeros((half,), bool)
    relay_in = by_parity(none, jnp.logical_not(direct_in))[:, None, None]
    drop_out = by_parity(none, jnp.logical_not(direct_out))[:, None, None]

    v = in_order(col_factors[0], 4 - col, 8 - col)
    u = in_order(row_factors[0][::-1], 3 - col, 7 - col)
    v_real, v_imag = (v[:, i].reshape(slots * levels, -1) for i in range(2))
    u_real, u_imag = (u[:, i].reshape(slots * levels, -1) for i in range(2))

    rank_table = ranks[0]
    my_ranks = lax.dynamic_index_in_dim(rank_table, myself, 0, keepdims=False)
    anchors = myself - (jnp.arange(slots, dtype=jnp.int32) - half)
    holder = jnp.arange(ntile, dtype=jnp.int32)[:, None] == anchors[None, :]
    row_ranks = jnp.sum(jnp.where(holder, rank_table, 0), axis=0)
    level_ids = jnp.arange(levels, dtype=jnp.int32)
    col_mask = (level_ids[None, :] < in_order(my_ranks, 4 - col, 8 - col)[:, None])[..., None]
    row_mask = (
        level_ids[None, :] < in_order(row_ranks[::-1], 3 - col, 7 - col)[:, None]
    )[..., None]

    gate_re, gate_im = gate_matrix(gate_window, nfreq)
    stepping = step_sizes[0]
    model = model_start[0]
    observed = data[0].astype(jnp.float32)
    width = model.shape[-1]
    part = model.shape[0] // nfreq

    def multiply(real, imag, values):
        return jnp.dot(real, values, preferred_element_type=jnp.float32) + jnp.dot(
            imag, rotate(values), preferred_element_type=jnp.float32
        )

    partner = None
    for step in range(ITERS):
        model_bf = model.astype(jnp.bfloat16)
        coef = multiply(v_real, v_imag, model_bf)
        coef = jnp.where(col_mask, coef.reshape(slots, levels, width), 0.0).astype(jnp.bfloat16)
        if step == 0:
            beyond = cross_half(coef)
            kept = jnp.where(cross_half(col_mask)[:, None], cross_half(v), 0)
            beyond, kept = lax.optimization_barrier((beyond, kept))
            far = swap(beyond)
            w = swap(kept)
            w_real, w_imag = (w[:, i].reshape(half * levels, -1) for i in range(2))
        else:
            far = multiply(w_real, w_imag, partner).astype(jnp.bfloat16)
            far = far.reshape(half, levels, width)
        direct, relayed = spread(coef, far)
        placed = jnp.where(relay_in, jnp.concatenate([relayed, relayed]), direct)
        placed = placed.reshape(slots * levels, width)
        image = left_dot(u_real, placed) + left_dot(u_imag, rotate(placed))
        resid = (image - observed).astype(jnp.bfloat16)
        back = jnp.dot(u_real, resid, preferred_element_type=jnp.float32) - jnp.dot(
            u_imag, rotate(resid), preferred_element_type=jnp.float32
        )
        back = jnp.where(row_mask, back.reshape(slots, levels, width), 0.0).astype(jnp.bfloat16)
        direct, relayed = spread(back, cross_half(back))
        landed = jnp.where(drop_out, 0, direct).reshape(slots * levels, width)
        handed = jnp.where(direct_out[:, None, None], relayed, 0).reshape(half * levels, width)
        grad = left_dot(v_real, landed) - left_dot(v_imag, rotate(landed))
        share = left_dot(w_real, handed) - left_dot(w_imag, rotate(handed))
        mine = (model - stepping * grad).astype(jnp.bfloat16).reshape(nfreq, part, width)
        theirs = (-stepping * share).astype(jnp.bfloat16).reshape(nfreq, part, width)
        both = jnp.where(
            odd, jnp.stack([mine, theirs], axis=1), jnp.stack([theirs, mine], axis=1)
        )
        z = jnp.sum(among_pair(both).astype(jnp.float32), axis=1)
        mixed = complex_mix(gate_re, gate_im, z).astype(jnp.bfloat16)
        if step == ITERS - 1:
            model = lax.all_to_all(mixed, "freq", 0, 0, tiled=True)
            model = model.astype(jnp.float32).reshape(nfreq * part, width)
        else:
            pair = among_pair(jnp.stack([mixed, mixed], axis=1))
            low = pair[:, 0].reshape(nfreq * part, width)
            high = pair[:, 1].reshape(nfreq * part, width)
            model = jnp.where(odd, low, high).astype(jnp.float32)
            partner = jnp.where(odd, high, low)
    return model[None]


def solution(mesh):
    return jax.shard_map(
        on_device,
        mesh=mesh,
        in_specs=(
            P("freq", "tile", None),
            P("freq", "tile", None),
            P("freq", "tile", None, None, None),
            P("freq", "tile", None, None, None),
            P("freq", None, None),
            P(),
            P("freq"),
        ),
        out_specs=P("freq", "tile", None),
        check_vma=False,
    )
```

```python
import functools
import math

import jax
import jax.numpy as jnp
from jax import lax
from jax.experimental import pallas as pl
from jax.experimental.pallas import tpu as pltpu
from jax.sharding import PartitionSpec as P

NT = 2048
ITERS = 2
WIDE = 4
VMEM_BYTES = 24 * 2**20
COL, ODD, OWN, FAR, ROW, SCALARS = 0, 1, 2, 10, 14, 24


def gate_matrix(window, count):
    start = window[:, 0].astype(jnp.float32)
    span = (window[:, 1] - window[:, 0]).astype(jnp.float32)
    freqs = jnp.arange(count, dtype=jnp.float32)
    delta = freqs[:, None] - freqs[None, :]
    theta = 2.0 * math.pi * delta / NT
    safe = jnp.where(delta == 0.0, 1.0, jnp.sin(theta / 2.0))
    magnitude = jnp.where(
        (delta == 0.0)[:, :, None],
        span[None, None, :] / NT,
        jnp.sin(theta[:, :, None] * span[None, None, :] / 2.0) / (NT * safe[:, :, None]),
    )
    phase = theta[:, :, None] * (start[None, None, :] + (span[None, None, :] - 1.0) / 2.0)
    return (magnitude * jnp.cos(phase), magnitude * jnp.sin(phase))


def turn(z):
    width = z.shape[-1]
    lane = lax.broadcasted_iota(jnp.int32, z.shape, z.ndim - 1)
    rolled = pltpu.roll(z, width // 2, z.ndim - 1)
    return jnp.where(lane < width // 2, -rolled, rolled)


def turn_bf(z):
    return turn(z.astype(jnp.float32)).astype(jnp.bfloat16)


def dot(a, b):
    return jnp.dot(a, b, preferred_element_type=jnp.float32)


def left_dot(a, b):
    return lax.dot_general(a, b, (((0,), (0,)), ((), ())), preferred_element_type=jnp.float32)


def keep(value, rank):
    row = lax.broadcasted_iota(jnp.int32, value.shape, 0)
    return jnp.where(row < rank, value.astype(jnp.float32), 0.0).astype(jnp.bfloat16)


def side_of(ref, side):
    return jnp.concatenate([ref[j, side] for j in range(ref.shape[0])], axis=0)


def far_factor(far_ref, index, which, levels):
    start = (2 * index + which) * levels
    return far_ref[start : start + levels, :]


def outward(col, s, odd):
    column = (col + s) & 3
    way = (col + s) >> 2
    same = way == 1
    near = jnp.where(odd == 1, way == 0, way == 2)
    return column, same, near


def coef_kernel(scal, v_ref, far_ref, x_ref, out_ref, *, first):
    slots, _, levels, rows = v_ref.shape
    half = slots // 2
    col, odd = scal[COL], scal[ODD]
    if first:
        x = x_ref[...].astype(jnp.bfloat16)
        packed = far_ref[half * 2 * levels :, :]
        width = x.shape[-1]
        x_far = jnp.concatenate([packed[:, :width], packed[:, width:]], axis=0)
    else:
        x = side_of(x_ref, 1 - odd)
        x_far = side_of(x_ref, odd)
    x_turn, far_turn = turn_bf(x), turn_bf(x_far)
    for s in range(slots):
        column, same, _ = outward(col, s, odd)
        place = column + half * jnp.where(same, odd, 1 - odd)
        out_ref[place, 0] = keep(dot(v_ref[s, 0], x) + dot(v_ref[s, 1], x_turn), scal[OWN + s])
    for i in range(half):
        column = (col + i) & 3
        piece = dot(far_factor(far_ref, i, 0, levels), x_far)
        piece += dot(far_factor(far_ref, i, 1, levels), far_turn)
        piece = keep(piece, scal[FAR + i])
        out_ref[column, 1] = piece
        out_ref[column + half, 1] = piece


def resid_kernel(scal, got_ref, u_ref, data_ref, out_ref):
    slots = u_ref.shape[0]
    half = slots // 2
    col, odd = scal[COL], scal[ODD]
    real = jnp.zeros(data_ref.shape, jnp.float32)
    imag = jnp.zeros(data_ref.shape, jnp.float32)
    for s in range(slots):
        column = (col + slots - s) & 3
        way = (col + slots - s) >> 2
        near = jnp.where(odd == 1, way == 0, way == 2)
        relay = jnp.logical_not(jnp.logical_or(near, way == 1)).astype(jnp.int32)
        piece = got_ref[column + half * jnp.where(near, 1 - odd, odd), relay]
        real += left_dot(u_ref[s, 0], piece)
        imag += left_dot(u_ref[s, 1], piece)
    image = real + turn(imag)
    resid = (image - data_ref[...].astype(jnp.float32)).astype(jnp.bfloat16)
    resid_turn = turn_bf(resid)
    for s in range(slots):
        column = (col + slots - s) & 3
        same = ((col + slots - s) >> 2) == 1
        piece = keep(dot(u_ref[s, 0], resid) - dot(u_ref[s, 1], resid_turn), scal[ROW + s])
        out_ref[column + half * jnp.where(same, odd, 1 - odd), 0] = piece

        @pl.when(jnp.logical_not(same))
        def _():
            out_ref[column, 1] = piece
            out_ref[column + half, 1] = piece


def grad_kernel(scal, size_ref, got_ref, v_ref, far_ref, x_ref, out_ref, *, first):
    slots, _, levels, _ = v_ref.shape
    half = slots // 2
    col, odd = scal[COL], scal[ODD]
    parts, _, part, width = out_ref.shape
    shape = (parts * part, width)
    real = jnp.zeros(shape, jnp.float32)
    imag = jnp.zeros(shape, jnp.float32)
    for s in range(slots):
        column, same, near = outward(col, s, odd)
        piece = got_ref[column + half * jnp.where(same, odd, 1 - odd), 0]
        piece = keep(piece, jnp.where(jnp.logical_or(same, near), levels, 0))
        real += left_dot(v_ref[s, 0], piece)
        imag += left_dot(v_ref[s, 1], piece)
    far_real = jnp.zeros(shape, jnp.float32)
    far_imag = jnp.zeros(shape, jnp.float32)
    for i in range(half):
        column = (col + i) & 3
        valid = (col + i < half).astype(jnp.int32) == odd
        piece = keep(got_ref[column + half * odd, 1], jnp.where(valid, levels, 0))
        far_real += left_dot(far_factor(far_ref, i, 0, levels), piece)
        far_imag += left_dot(far_factor(far_ref, i, 1, levels), piece)
    x = x_ref[...] if first else side_of(x_ref, 1 - odd).astype(jnp.float32)
    size = size_ref[0]
    mine = (x - size * (real - turn(imag))).astype(jnp.bfloat16)
    theirs = (-size * (far_real - turn(far_imag))).astype(jnp.bfloat16)
    for j in range(parts):
        out_ref[j, 1 - odd] = mine[j * part : (j + 1) * part]
        out_ref[j, odd] = theirs[j * part : (j + 1) * part]


def mix_kernel(re_ref, im_ref, got_ref, out_ref):
    count = got_ref.shape[0]
    z, z_turn = [], []
    for g in range(count):
        total = got_ref[g, 0].astype(jnp.float32) + got_ref[g, 1].astype(jnp.float32)
        z.append(total)
        z_turn.append(turn(total))
    for f in range(count):
        total = jnp.zeros_like(z[0])
        for g in range(count):
            total += re_ref[f, g : g + 1, :] * z[g] + im_ref[f, g : g + 1, :] * z_turn[g]
        total = total.astype(jnp.bfloat16)
        for side in range(out_ref.shape[1]):
            out_ref[f, side] = total


def kernel_call(body, shape, scalars, *operands):
    smem = pl.BlockSpec(memory_space=pltpu.SMEM)
    vmem = pl.BlockSpec(memory_space=pltpu.VMEM)
    return pl.pallas_call(
        body,
        out_shape=jax.ShapeDtypeStruct(shape, jnp.bfloat16),
        in_specs=[smem] * len(scalars) + [vmem] * len(operands),
        out_specs=vmem,
        compiler_params=pltpu.CompilerParams(vmem_limit_bytes=VMEM_BYTES),
    )(*scalars, *operands)


def on_device(model_start, data, col_factors, row_factors, ranks, gate_window, step_sizes):
    ntile = lax.axis_size("tile")
    nfreq = lax.axis_size("freq")
    myself = lax.axis_index("tile")
    slots = ranks.shape[2]
    levels = col_factors.shape[3]
    half = slots // 2
    rows_z = ntile // WIDE
    col = myself % WIDE
    odd = (myself // WIDE) % 2
    groups = [[slots * k + i for i in range(slots)] for k in range(ntile // slots)]
    swaps = [
        (z * WIDE + y, (z + 1 if z % 2 else z - 1) * WIDE + y)
        for z in range(1, rows_z - 1)
        for y in range(WIDE)
    ]
    pairs = [
        [
            f * ntile + (z % rows_z) * WIDE + y
            for f in range(nfreq)
            for z in (2 * k - 1, 2 * k)
        ]
        for k in range(rows_z // 2)
        for y in range(WIDE)
    ]

    def spread(pieces):
        return lax.all_to_all(pieces, "tile", 0, 0, tiled=True, axis_index_groups=groups)

    def among_pair(pieces):
        flat = pieces.reshape(2 * nfreq, -1, pieces.shape[-1])
        got = lax.all_to_all(
            flat, ("freq", "tile"), 0, 0, tiled=True, axis_index_groups=pairs
        )
        return got.reshape(pieces.shape)

    model = model_start[0]
    rows, width = model.shape
    part = rows // nfreq
    v, u, observed = col_factors[0], row_factors[0], data[0]

    beyond = lax.dynamic_slice_in_dim(v, half * odd, half, 0).reshape(-1, rows)
    start = model.astype(jnp.bfloat16)
    start = jnp.concatenate([start[: rows // 2], start[rows // 2 :]], axis=1)
    far = lax.ppermute(jnp.concatenate([beyond, start], axis=0), "tile", swaps)

    table = ranks[0]
    slot_ids = jnp.arange(slots, dtype=jnp.int32)
    opposite = jnp.clip(myself + jnp.where(odd == 1, WIDE, -WIDE), 0, ntile - 1)
    far_ranks = lax.dynamic_slice(table, (opposite, half * (1 - odd)), (1, half))[0]
    own_ranks = lax.dynamic_index_in_dim(table, myself, 0, keepdims=False)
    anchors = jnp.clip(myself + half - slot_ids, 0, ntile - 1)
    holder = jnp.arange(ntile, dtype=jnp.int32)[:, None] == anchors[None, :]
    row_ranks = jnp.sum(jnp.where(holder, table, 0), axis=0)
    scal = jnp.concatenate([jnp.stack([col, odd]), own_ranks, far_ranks, row_ranks])
    scal = jnp.pad(scal, (0, SCALARS - scal.shape[0]))

    gate_re, gate_im = gate_matrix(gate_window, nfreq)
    gate_re = jnp.concatenate([gate_re, gate_re], axis=-1)
    gate_im = jnp.concatenate([gate_im, gate_im], axis=-1)

    tiles = (slots, 2, levels, width)
    for step in range(ITERS):
        first = step == 0
        coef = kernel_call(
            functools.partial(coef_kernel, first=first), tiles, [scal], v, far, model
        )
        back = kernel_call(resid_kernel, tiles, [scal], spread(coef), u, observed)
        z = kernel_call(
            functools.partial(grad_kernel, first=first),
            (nfreq, 2, part, width),
            [scal, step_sizes],
            spread(back),
            v,
            far,
            model,
        )
        z = among_pair(z)
        if step == ITERS - 1:
            mixed = kernel_call(mix_kernel, (nfreq, 1, part, width), [], gate_re, gate_im, z)
            model = lax.all_to_all(mixed[:, 0], "freq", 0, 0, tiled=True)
        else:
            mixed = kernel_call(mix_kernel, z.shape, [], gate_re, gate_im, z)
            model = among_pair(mixed)
    return model.reshape(1, rows, width).astype(jnp.float32)


def solution(mesh):
    return jax.shard_map(
        on_device,
        mesh=mesh,
        in_specs=(
            P("freq", "tile", None),
            P("freq", "tile", None),
            P("freq", "tile", None, None, None),
            P("freq", "tile", None, None, None),
            P("freq", None, None),
            P(),
            P("freq"),
        ),
        out_specs=P("freq", "tile", None),
        check_vma=False,
    )
```

```python
import functools
import math

import jax
import jax.numpy as jnp
from jax import lax
from jax.experimental import pallas as pl
from jax.experimental.pallas import tpu as pltpu
from jax.sharding import PartitionSpec as P

NT = 2048
ITERS = 2
WIDE = 4
VMEM_BYTES = 24 * 2**20
COL, ODD, OWN, FAR, ROW, SCALARS = 0, 1, 2, 10, 14, 24


def gate_matrix(window, count):
    start = window[:, 0].astype(jnp.float32)
    span = (window[:, 1] - window[:, 0]).astype(jnp.float32)
    freqs = jnp.arange(count, dtype=jnp.float32)
    delta = freqs[:, None] - freqs[None, :]
    theta = 2.0 * math.pi * delta / NT
    safe = jnp.where(delta == 0.0, 1.0, jnp.sin(theta / 2.0))
    magnitude = jnp.where(
        (delta == 0.0)[:, :, None],
        span[None, None, :] / NT,
        jnp.sin(theta[:, :, None] * span[None, None, :] / 2.0) / (NT * safe[:, :, None]),
    )
    phase = theta[:, :, None] * (start[None, None, :] + (span[None, None, :] - 1.0) / 2.0)
    return (magnitude * jnp.cos(phase), magnitude * jnp.sin(phase))


def turn(z):
    width = z.shape[-1]
    lane = lax.broadcasted_iota(jnp.int32, z.shape, z.ndim - 1)
    rolled = pltpu.roll(z, width // 2, z.ndim - 1)
    return jnp.where(lane < width // 2, -rolled, rolled)


def turn_bf(z):
    return turn(z.astype(jnp.float32)).astype(jnp.bfloat16)


def dot(a, b):
    return jnp.dot(a, b, preferred_element_type=jnp.float32)


def left_dot(a, b):
    return lax.dot_general(a, b, (((0,), (0,)), ((), ())), preferred_element_type=jnp.float32)


def keep(value, rank):
    row = lax.broadcasted_iota(jnp.int32, value.shape, 0)
    return jnp.where(row < rank, value.astype(jnp.float32), 0.0).astype(jnp.bfloat16)


def side_of(ref, side):
    return jnp.concatenate([ref[j, side] for j in range(ref.shape[0])], axis=0)


def far_factor(far_refs, index, which):
    each = far_refs[0].shape[0]
    return far_refs[index // each][index % each, which]


def outward(col, s, odd):
    column = (col + s) & 3
    way = (col + s) >> 2
    same = way == 1
    near = jnp.where(odd == 1, way == 0, way == 2)
    return column, same, near


def beyond_kernel(scal, v_ref, x_ref, out_ref):
    half = out_ref.shape[0]
    x = x_ref[...].astype(jnp.bfloat16)
    x_turn = turn_bf(x)
    for i in range(half):
        s = half * scal[ODD] + i
        out_ref[i] = (dot(v_ref[s, 0], x) + dot(v_ref[s, 1], x_turn)).astype(jnp.bfloat16)


def own_coefs(scal, v_ref, x, out_ref):
    slots = v_ref.shape[0]
    half = slots // 2
    col, odd = scal[COL], scal[ODD]
    x_turn = turn_bf(x)
    for s in range(slots):
        column, same, _ = outward(col, s, odd)
        place = column + half * jnp.where(same, odd, 1 - odd)
        out_ref[place, 0] = keep(dot(v_ref[s, 0], x) + dot(v_ref[s, 1], x_turn), scal[OWN + s])


def first_coef_kernel(scal, v_ref, x_ref, relay_ref, out_ref):
    half = relay_ref.shape[0]
    own_coefs(scal, v_ref, x_ref[...].astype(jnp.bfloat16), out_ref)
    for i in range(half):
        column = (scal[COL] + i) & 3
        piece = keep(relay_ref[i], scal[FAR + i])
        out_ref[column, 1] = piece
        out_ref[column + half, 1] = piece


def coef_kernel(scal, v_ref, near_far_ref, last_far_ref, x_ref, out_ref):
    half = v_ref.shape[0] // 2
    odd = scal[ODD]
    far_refs = (near_far_ref, last_far_ref)
    x_far = side_of(x_ref, odd)
    far_turn = turn_bf(x_far)
    own_coefs(scal, v_ref, side_of(x_ref, 1 - odd), out_ref)
    for i in range(half):
        column = (scal[COL] + i) & 3
        piece = dot(far_factor(far_refs, i, 0), x_far) + dot(far_factor(far_refs, i, 1), far_turn)
        piece = keep(piece, scal[FAR + i])
        out_ref[column, 1] = piece
        out_ref[column + half, 1] = piece


def resid_kernel(scal, got_ref, u_ref, data_ref, *rest):
    out_ref = rest[-1]
    slots = u_ref.shape[0]
    half = slots // 2
    col, odd = scal[COL], scal[ODD]
    real = jnp.zeros(data_ref.shape, jnp.float32)
    imag = jnp.zeros(data_ref.shape, jnp.float32)
    for s in range(slots):
        column = (col + slots - s) & 3
        way = (col + slots - s) >> 2
        near = jnp.where(odd == 1, way == 0, way == 2)
        relay = jnp.logical_not(jnp.logical_or(near, way == 1)).astype(jnp.int32)
        piece = got_ref[column + half * jnp.where(near, 1 - odd, odd), relay]
        real += left_dot(u_ref[s, 0], piece)
        imag += left_dot(u_ref[s, 1], piece)
    image = real + turn(imag)
    resid = (image - data_ref[...].astype(jnp.float32)).astype(jnp.bfloat16)
    resid_turn = turn_bf(resid)
    for s in range(slots):
        column = (col + slots - s) & 3
        same = ((col + slots - s) >> 2) == 1
        piece = keep(dot(u_ref[s, 0], resid) - dot(u_ref[s, 1], resid_turn), scal[ROW + s])
        out_ref[column + half * jnp.where(same, odd, 1 - odd), 0] = piece

        @pl.when(jnp.logical_not(same))
        def _():
            out_ref[column, 1] = piece
            out_ref[column + half, 1] = piece


def grad_kernel(
    scal, size_ref, got_ref, v_ref, near_far_ref, last_far_ref, x_ref, out_ref, *, first
):
    far_refs = (near_far_ref, last_far_ref)
    slots, _, levels, _ = v_ref.shape
    half = slots // 2
    col, odd = scal[COL], scal[ODD]
    parts, _, part, width = out_ref.shape
    shape = (parts * part, width)
    real = jnp.zeros(shape, jnp.float32)
    imag = jnp.zeros(shape, jnp.float32)
    for s in range(slots):
        column, same, near = outward(col, s, odd)
        piece = got_ref[column + half * jnp.where(same, odd, 1 - odd), 0]
        piece = keep(piece, jnp.where(jnp.logical_or(same, near), levels, 0))
        real += left_dot(v_ref[s, 0], piece)
        imag += left_dot(v_ref[s, 1], piece)
    far_real = jnp.zeros(shape, jnp.float32)
    far_imag = jnp.zeros(shape, jnp.float32)
    for i in range(half):
        column = (col + i) & 3
        valid = (col + i < half).astype(jnp.int32) == odd
        piece = keep(got_ref[column + half * odd, 1], jnp.where(valid, levels, 0))
        far_real += left_dot(far_factor(far_refs, i, 0), piece)
        far_imag += left_dot(far_factor(far_refs, i, 1), piece)
    x = x_ref[...] if first else side_of(x_ref, 1 - odd).astype(jnp.float32)
    size = size_ref[0]
    mine = (x - size * (real - turn(imag))).astype(jnp.bfloat16)
    theirs = (-size * (far_real - turn(far_imag))).astype(jnp.bfloat16)
    for j in range(parts):
        out_ref[j, 1 - odd] = mine[j * part : (j + 1) * part]
        out_ref[j, odd] = theirs[j * part : (j + 1) * part]


def mix_kernel(re_ref, im_ref, got_ref, out_ref):
    count = got_ref.shape[0]
    z, z_turn = [], []
    for g in range(count):
        total = got_ref[g, 0].astype(jnp.float32) + got_ref[g, 1].astype(jnp.float32)
        z.append(total)
        z_turn.append(turn(total))
    for f in range(count):
        total = jnp.zeros_like(z[0])
        for g in range(count):
            total += re_ref[f, g : g + 1, :] * z[g] + im_ref[f, g : g + 1, :] * z_turn[g]
        total = total.astype(jnp.bfloat16)
        for side in range(out_ref.shape[1]):
            out_ref[f, side] = total


def kernel_call(body, shape, scalars, *operands):
    smem = pl.BlockSpec(memory_space=pltpu.SMEM)
    vmem = pl.BlockSpec(memory_space=pltpu.VMEM)
    return pl.pallas_call(
        body,
        out_shape=jax.ShapeDtypeStruct(shape, jnp.bfloat16),
        in_specs=[smem] * len(scalars) + [vmem] * len(operands),
        out_specs=vmem,
        compiler_params=pltpu.CompilerParams(vmem_limit_bytes=VMEM_BYTES),
    )(*scalars, *operands)


def on_device(model_start, data, col_factors, row_factors, ranks, gate_window, step_sizes):
    ntile = lax.axis_size("tile")
    nfreq = lax.axis_size("freq")
    myself = lax.axis_index("tile")
    slots = ranks.shape[2]
    levels = col_factors.shape[3]
    half = slots // 2
    rows_z = ntile // WIDE
    col = myself % WIDE
    odd = (myself // WIDE) % 2
    groups = [[slots * k + i for i in range(slots)] for k in range(ntile // slots)]
    swaps = [
        (z * WIDE + y, (z + 1 if z % 2 else z - 1) * WIDE + y)
        for z in range(1, rows_z - 1)
        for y in range(WIDE)
    ]
    pairs = [
        [
            f * ntile + (z % rows_z) * WIDE + y
            for f in range(nfreq)
            for z in (2 * k - 1, 2 * k)
        ]
        for k in range(rows_z // 2)
        for y in range(WIDE)
    ]

    def spread(pieces):
        return lax.all_to_all(pieces, "tile", 0, 0, tiled=True, axis_index_groups=groups)

    def among_pair(pieces):
        flat = pieces.reshape(2 * nfreq, -1, pieces.shape[-1])
        got = lax.all_to_all(
            flat, ("freq", "tile"), 0, 0, tiled=True, axis_index_groups=pairs
        )
        return got.reshape(pieces.shape)

    model = model_start[0]
    rows, width = model.shape
    part = rows // nfreq
    v, u, observed = col_factors[0], row_factors[0], data[0]

    where = jnp.stack([col, odd])
    relay = kernel_call(beyond_kernel, (half, levels, width), [where], v, model)
    relay = lax.ppermute(relay, "tile", swaps)
    fars = [
        lax.ppermute(
            lax.dynamic_slice_in_dim(v, half * odd + i, half // 2, 0), "tile", swaps
        )
        for i in (0, half // 2)
    ]

    table = ranks[0]
    slot_ids = jnp.arange(slots, dtype=jnp.int32)
    opposite = jnp.clip(myself + jnp.where(odd == 1, WIDE, -WIDE), 0, ntile - 1)
    far_ranks = lax.dynamic_slice(table, (opposite, half * (1 - odd)), (1, half))[0]
    own_ranks = lax.dynamic_index_in_dim(table, myself, 0, keepdims=False)
    anchors = jnp.clip(myself + half - slot_ids, 0, ntile - 1)
    holder = jnp.arange(ntile, dtype=jnp.int32)[:, None] == anchors[None, :]
    row_ranks = jnp.sum(jnp.where(holder, table, 0), axis=0)
    scal = jnp.concatenate([where, own_ranks, far_ranks, row_ranks])
    scal = jnp.pad(scal, (0, SCALARS - scal.shape[0]))

    gate_re, gate_im = gate_matrix(gate_window, nfreq)
    gate_re = jnp.concatenate([gate_re, gate_re], axis=-1)
    gate_im = jnp.concatenate([gate_im, gate_im], axis=-1)

    tiles = (slots, 2, levels, width)
    for step in range(ITERS):
        first = step == 0
        if first:
            coef = kernel_call(first_coef_kernel, tiles, [scal], v, model, relay)
            back = kernel_call(resid_kernel, tiles, [scal], spread(coef), u, observed, fars[0])
        else:
            coef = kernel_call(coef_kernel, tiles, [scal], v, *fars, model)
            back = kernel_call(resid_kernel, tiles, [scal], spread(coef), u, observed)
        z = kernel_call(
            functools.partial(grad_kernel, first=first),
            (nfreq, 2, part, width),
            [scal, step_sizes],
            spread(back),
            v,
            *fars,
            model,
        )
        z = among_pair(z)
        if step == ITERS - 1:
            mixed = kernel_call(mix_kernel, (nfreq, 1, part, width), [], gate_re, gate_im, z)
            model = lax.all_to_all(mixed[:, 0], "freq", 0, 0, tiled=True)
        else:
            mixed = kernel_call(mix_kernel, z.shape, [], gate_re, gate_im, z)
            model = among_pair(mixed)
    return model.reshape(1, rows, width).astype(jnp.float32)


def solution(mesh):
    return jax.shard_map(
        on_device,
        mesh=mesh,
        in_specs=(
            P("freq", "tile", None),
            P("freq", "tile", None),
            P("freq", "tile", None, None, None),
            P("freq", "tile", None, None, None),
            P("freq", None, None),
            P(),
            P("freq"),
        ),
        out_specs=P("freq", "tile", None),
        check_vma=False,
    )
```

```python
import functools
import math

import jax
import jax.numpy as jnp
from jax import lax
from jax.experimental import pallas as pl
from jax.experimental.pallas import tpu as pltpu
from jax.sharding import PartitionSpec as P

NT = 2048
ITERS = 2
WIDE = 4
VMEM_BYTES = 24 * 2**20
COL, ODD, OWN, FAR, ROW, SCALARS = 0, 1, 2, 10, 14, 24


def gate_matrix(window, count):
    start = window[:, 0].astype(jnp.float32)
    span = (window[:, 1] - window[:, 0]).astype(jnp.float32)
    freqs = jnp.arange(count, dtype=jnp.float32)
    delta = freqs[:, None] - freqs[None, :]
    theta = 2.0 * math.pi * delta / NT
    safe = jnp.where(delta == 0.0, 1.0, jnp.sin(theta / 2.0))
    magnitude = jnp.where(
        (delta == 0.0)[:, :, None],
        span[None, None, :] / NT,
        jnp.sin(theta[:, :, None] * span[None, None, :] / 2.0) / (NT * safe[:, :, None]),
    )
    phase = theta[:, :, None] * (start[None, None, :] + (span[None, None, :] - 1.0) / 2.0)
    return (magnitude * jnp.cos(phase), magnitude * jnp.sin(phase))


def turn(z):
    width = z.shape[-1]
    lane = lax.broadcasted_iota(jnp.int32, z.shape, z.ndim - 1)
    rolled = pltpu.roll(z, width // 2, z.ndim - 1)
    return jnp.where(lane < width // 2, -rolled, rolled)


def turn_bf(z):
    return turn(z.astype(jnp.float32)).astype(jnp.bfloat16)


def dot(a, b):
    return jnp.dot(a, b, preferred_element_type=jnp.float32)


def left_dot(a, b):
    return lax.dot_general(a, b, (((0,), (0,)), ((), ())), preferred_element_type=jnp.float32)


def keep(value, rank):
    row = lax.broadcasted_iota(jnp.int32, value.shape, 0)
    return jnp.where(row < rank, value.astype(jnp.float32), 0.0).astype(jnp.bfloat16)


def side_of(ref, side):
    return jnp.concatenate([ref[j, side] for j in range(ref.shape[0])], axis=0)


def far_factor(far_refs, index, which):
    each = far_refs[0].shape[0]
    return far_refs[index // each][index % each, which]


def outward(col, s, odd):
    column = (col + s) & 3
    way = (col + s) >> 2
    same = way == 1
    near = jnp.where(odd == 1, way == 0, way == 2)
    return column, same, near


def beyond_kernel(scal, v_ref, x_ref, out_ref, *far_refs):
    half = out_ref.shape[0]
    each = far_refs[0].shape[0]
    x = x_ref[...].astype(jnp.bfloat16)
    x_turn = turn_bf(x)
    for i in range(half):
        s = half * scal[ODD] + i
        out_ref[i] = (dot(v_ref[s, 0], x) + dot(v_ref[s, 1], x_turn)).astype(jnp.bfloat16)
        far_refs[i // each][i % each] = v_ref[s]


def own_coefs(scal, v_ref, x, out_ref):
    slots = v_ref.shape[0]
    half = slots // 2
    col, odd = scal[COL], scal[ODD]
    x_turn = turn_bf(x)
    for s in range(slots):
        column, same, _ = outward(col, s, odd)
        place = column + half * jnp.where(same, odd, 1 - odd)
        out_ref[place, 0] = keep(dot(v_ref[s, 0], x) + dot(v_ref[s, 1], x_turn), scal[OWN + s])


def first_coef_kernel(scal, v_ref, x_ref, relay_ref, out_ref):
    half = relay_ref.shape[0]
    own_coefs(scal, v_ref, x_ref[...].astype(jnp.bfloat16), out_ref)
    for i in range(half):
        column = (scal[COL] + i) & 3
        piece = keep(relay_ref[i], scal[FAR + i])
        out_ref[column, 1] = piece
        out_ref[column + half, 1] = piece


def coef_kernel(scal, v_ref, near_far_ref, last_far_ref, x_ref, out_ref):
    half = v_ref.shape[0] // 2
    odd = scal[ODD]
    far_refs = (near_far_ref, last_far_ref)
    x_far = side_of(x_ref, odd)
    far_turn = turn_bf(x_far)
    own_coefs(scal, v_ref, side_of(x_ref, 1 - odd), out_ref)
    for i in range(half):
        column = (scal[COL] + i) & 3
        piece = dot(far_factor(far_refs, i, 0), x_far) + dot(far_factor(far_refs, i, 1), far_turn)
        piece = keep(piece, scal[FAR + i])
        out_ref[column, 1] = piece
        out_ref[column + half, 1] = piece


def resid_kernel(scal, got_ref, u_ref, data_ref, *rest):
    out_ref = rest[-1]
    slots = u_ref.shape[0]
    half = slots // 2
    col, odd = scal[COL], scal[ODD]
    real = jnp.zeros(data_ref.shape, jnp.float32)
    imag = jnp.zeros(data_ref.shape, jnp.float32)
    for s in range(slots):
        column = (col + slots - s) & 3
        way = (col + slots - s) >> 2
        near = jnp.where(odd == 1, way == 0, way == 2)
        relay = jnp.logical_not(jnp.logical_or(near, way == 1)).astype(jnp.int32)
        piece = got_ref[column + half * jnp.where(near, 1 - odd, odd), relay]
        real += left_dot(u_ref[s, 0], piece)
        imag += left_dot(u_ref[s, 1], piece)
    image = real + turn(imag)
    resid = (image - data_ref[...].astype(jnp.float32)).astype(jnp.bfloat16)
    resid_turn = turn_bf(resid)
    for s in range(slots):
        column = (col + slots - s) & 3
        same = ((col + slots - s) >> 2) == 1
        piece = keep(dot(u_ref[s, 0], resid) - dot(u_ref[s, 1], resid_turn), scal[ROW + s])
        place = column + half * jnp.where(same, odd, 1 - odd)
        out_ref[place, 0] = piece
        out_ref[(place + half) & (slots - 1), 1] = piece


def grad_kernel(
    scal, size_ref, got_ref, v_ref, near_far_ref, last_far_ref, x_ref, out_ref, *, first
):
    far_refs = (near_far_ref, last_far_ref)
    slots, _, levels, _ = v_ref.shape
    half = slots // 2
    col, odd = scal[COL], scal[ODD]
    parts, _, part, width = out_ref.shape
    shape = (parts * part, width)
    real = jnp.zeros(shape, jnp.float32)
    imag = jnp.zeros(shape, jnp.float32)
    for s in range(slots):
        column, same, near = outward(col, s, odd)
        piece = got_ref[column + half * jnp.where(same, odd, 1 - odd), 0]
        piece = keep(piece, jnp.where(jnp.logical_or(same, near), levels, 0))
        real += left_dot(v_ref[s, 0], piece)
        imag += left_dot(v_ref[s, 1], piece)
    far_real = jnp.zeros(shape, jnp.float32)
    far_imag = jnp.zeros(shape, jnp.float32)
    for i in range(half):
        column = (col + i) & 3
        valid = (col + i < half).astype(jnp.int32) == odd
        piece = keep(got_ref[column + half * odd, 1], jnp.where(valid, levels, 0))
        far_real += left_dot(far_factor(far_refs, i, 0), piece)
        far_imag += left_dot(far_factor(far_refs, i, 1), piece)
    x = x_ref[...] if first else side_of(x_ref, 1 - odd).astype(jnp.float32)
    size = size_ref[0]
    mine = (x - size * (real - turn(imag))).astype(jnp.bfloat16)
    theirs = (-size * (far_real - turn(far_imag))).astype(jnp.bfloat16)
    for j in range(parts):
        out_ref[j, 1 - odd] = mine[j * part : (j + 1) * part]
        out_ref[j, odd] = theirs[j * part : (j + 1) * part]


def mix_kernel(re_ref, im_ref, got_ref, out_ref):
    count = got_ref.shape[0]
    z, z_turn = [], []
    for g in range(count):
        total = got_ref[g, 0].astype(jnp.float32) + got_ref[g, 1].astype(jnp.float32)
        z.append(total)
        z_turn.append(turn(total))
    for f in range(count):
        total = jnp.zeros_like(z[0])
        for g in range(count):
            total += re_ref[f, g : g + 1, :] * z[g] + im_ref[f, g : g + 1, :] * z_turn[g]
        total = total.astype(jnp.bfloat16)
        for side in range(out_ref.shape[1]):
            out_ref[f, side] = total


def kernel_call(body, shape, scalars, *operands):
    smem = pl.BlockSpec(memory_space=pltpu.SMEM)
    vmem = pl.BlockSpec(memory_space=pltpu.VMEM)
    several = isinstance(shape, list)
    outs = [jax.ShapeDtypeStruct(s, jnp.bfloat16) for s in (shape if several else [shape])]
    return pl.pallas_call(
        body,
        out_shape=outs if several else outs[0],
        in_specs=[smem] * len(scalars) + [vmem] * len(operands),
        out_specs=[vmem] * len(outs) if several else vmem,
        compiler_params=pltpu.CompilerParams(vmem_limit_bytes=VMEM_BYTES),
    )(*scalars, *operands)


def on_device(model_start, data, col_factors, row_factors, ranks, gate_window, step_sizes):
    ntile = lax.axis_size("tile")
    nfreq = lax.axis_size("freq")
    myself = lax.axis_index("tile")
    slots = ranks.shape[2]
    levels = col_factors.shape[3]
    half = slots // 2
    rows_z = ntile // WIDE
    col = myself % WIDE
    odd = (myself // WIDE) % 2
    groups = [[slots * k + i for i in range(slots)] for k in range(ntile // slots)]
    swaps = [
        (z * WIDE + y, (z + 1 if z % 2 else z - 1) * WIDE + y)
        for z in range(1, rows_z - 1)
        for y in range(WIDE)
    ]
    pairs = [
        [
            f * ntile + (z % rows_z) * WIDE + y
            for f in range(nfreq)
            for z in (2 * k - 1, 2 * k)
        ]
        for k in range(rows_z // 2)
        for y in range(WIDE)
    ]

    def spread(pieces):
        return lax.all_to_all(pieces, "tile", 0, 0, tiled=True, axis_index_groups=groups)

    def among_pair(pieces):
        flat = pieces.reshape(2 * nfreq, -1, pieces.shape[-1])
        got = lax.all_to_all(
            flat, ("freq", "tile"), 0, 0, tiled=True, axis_index_groups=pairs
        )
        return got.reshape(pieces.shape)

    model = model_start[0]
    rows, width = model.shape
    part = rows // nfreq
    v, u, observed = col_factors[0], row_factors[0], data[0]

    where = jnp.stack([col, odd])
    relay, *fars = kernel_call(
        beyond_kernel,
        [(half, levels, width)] + [(half // 2, 2, levels, rows)] * 2,
        [where],
        v,
        model,
    )
    relay = lax.ppermute(relay, "tile", swaps)
    fars = [lax.ppermute(far, "tile", swaps) for far in fars]

    table = ranks[0]
    slot_ids = jnp.arange(slots, dtype=jnp.int32)
    opposite = jnp.clip(myself + jnp.where(odd == 1, WIDE, -WIDE), 0, ntile - 1)
    far_ranks = lax.dynamic_slice(table, (opposite, half * (1 - odd)), (1, half))[0]
    own_ranks = lax.dynamic_index_in_dim(table, myself, 0, keepdims=False)
    anchors = jnp.clip(myself + half - slot_ids, 0, ntile - 1)
    holder = jnp.arange(ntile, dtype=jnp.int32)[:, None] == anchors[None, :]
    row_ranks = jnp.sum(jnp.where(holder, table, 0), axis=0)
    scal = jnp.concatenate([where, own_ranks, far_ranks, row_ranks])
    scal = jnp.pad(scal, (0, SCALARS - scal.shape[0]))

    gate_re, gate_im = gate_matrix(gate_window, nfreq)
    gate_re = jnp.concatenate([gate_re, gate_re], axis=-1)
    gate_im = jnp.concatenate([gate_im, gate_im], axis=-1)

    tiles = (slots, 2, levels, width)
    for step in range(ITERS):
        first = step == 0
        if first:
            coef = kernel_call(first_coef_kernel, tiles, [scal], v, model, relay)
            back = kernel_call(resid_kernel, tiles, [scal], spread(coef), u, observed, fars[0])
        else:
            coef = kernel_call(coef_kernel, tiles, [scal], v, *fars, model)
            back = kernel_call(resid_kernel, tiles, [scal], spread(coef), u, observed)
        z = kernel_call(
            functools.partial(grad_kernel, first=first),
            (nfreq, 2, part, width),
            [scal, step_sizes],
            spread(back),
            v,
            *fars,
            model,
        )
        z = among_pair(z)
        if step == ITERS - 1:
            mixed = kernel_call(mix_kernel, (nfreq, 1, part, width), [], gate_re, gate_im, z)
            model = lax.all_to_all(mixed[:, 0], "freq", 0, 0, tiled=True)
        else:
            mixed = kernel_call(mix_kernel, z.shape, [], gate_re, gate_im, z)
            model = among_pair(mixed)
    return model.reshape(1, rows, width).astype(jnp.float32)


def solution(mesh):
    return jax.shard_map(
        on_device,
        mesh=mesh,
        in_specs=(
            P("freq", "tile", None),
            P("freq", "tile", None),
            P("freq", "tile", None, None, None),
            P("freq", "tile", None, None, None),
            P("freq", None, None),
            P(),
            P("freq"),
        ),
        out_specs=P("freq", "tile", None),
        check_vma=False,
    )
```

```python
import functools
import math

import jax
import jax.numpy as jnp
from jax import lax
from jax.experimental import pallas as pl
from jax.experimental.pallas import tpu as pltpu
from jax.sharding import PartitionSpec as P

NT = 2048
ITERS = 2
WIDE = 4
VMEM_BYTES = 24 * 2**20
FIRST_VMEM_BYTES = 62 * 2**20
COL, ODD, OWN, FAR, ROW, SCALARS = 0, 1, 2, 10, 14, 24


def gate_matrix(window, count):
    start = window[:, 0].astype(jnp.float32)
    span = (window[:, 1] - window[:, 0]).astype(jnp.float32)
    freqs = jnp.arange(count, dtype=jnp.float32)
    delta = freqs[:, None] - freqs[None, :]
    theta = 2.0 * math.pi * delta / NT
    safe = jnp.where(delta == 0.0, 1.0, jnp.sin(theta / 2.0))
    magnitude = jnp.where(
        (delta == 0.0)[:, :, None],
        span[None, None, :] / NT,
        jnp.sin(theta[:, :, None] * span[None, None, :] / 2.0) / (NT * safe[:, :, None]),
    )
    phase = theta[:, :, None] * (start[None, None, :] + (span[None, None, :] - 1.0) / 2.0)
    return (magnitude * jnp.cos(phase), magnitude * jnp.sin(phase))


def turn(z):
    width = z.shape[-1]
    lane = lax.broadcasted_iota(jnp.int32, z.shape, z.ndim - 1)
    rolled = pltpu.roll(z, width // 2, z.ndim - 1)
    return jnp.where(lane < width // 2, -rolled, rolled)


def turn_bf(z):
    return turn(z.astype(jnp.float32)).astype(jnp.bfloat16)


def dot(a, b):
    return jnp.dot(a, b, preferred_element_type=jnp.float32)


def left_dot(a, b):
    return lax.dot_general(a, b, (((0,), (0,)), ((), ())), preferred_element_type=jnp.float32)


def keep(value, rank):
    row = lax.broadcasted_iota(jnp.int32, value.shape, 0)
    return jnp.where(row < rank, value.astype(jnp.float32), 0.0).astype(jnp.bfloat16)


def side_of(ref, side):
    return jnp.concatenate([ref[j, side] for j in range(ref.shape[0])], axis=0)


def far_factor(far_refs, index, which):
    each = far_refs[0].shape[0]
    return far_refs[index // each][index % each, which]


def outward(col, s, odd):
    column = (col + s) & 3
    way = (col + s) >> 2
    same = way == 1
    near = jnp.where(odd == 1, way == 0, way == 2)
    return column, same, near


def beyond_kernel(scal, v_ref, x_ref, out_ref, low_ref, high_ref, x_here, arrived):
    half = out_ref.shape[0]
    each = half // 2
    copies = [pltpu.make_async_copy(x_ref, x_here, arrived.at[half])]
    for i in range(half):
        there = (low_ref, high_ref)[i // each].at[i % each]
        copies.append(pltpu.make_async_copy(v_ref.at[half * scal[ODD] + i], there, arrived.at[i]))
    for copy in copies:
        copy.start()
    copies[0].wait()
    x = x_here[...].astype(jnp.bfloat16)
    x_turn = turn_bf(x)
    for i in range(half):
        copies[1 + i].wait()
        tile = (low_ref, high_ref)[i // each]
        piece = dot(tile[i % each, 0], x) + dot(tile[i % each, 1], x_turn)
        out_ref[i] = piece.astype(jnp.bfloat16)


def own_coefs(scal, v_ref, x, out_ref):
    slots = v_ref.shape[0]
    half = slots // 2
    col, odd = scal[COL], scal[ODD]
    x_turn = turn_bf(x)
    for s in range(slots):
        column, same, _ = outward(col, s, odd)
        place = column + half * jnp.where(same, odd, 1 - odd)
        out_ref[place, 0] = keep(dot(v_ref[s, 0], x) + dot(v_ref[s, 1], x_turn), scal[OWN + s])


def first_coef_kernel(scal, v_ref, x_ref, relay_ref, out_ref):
    half = relay_ref.shape[0]
    own_coefs(scal, v_ref, x_ref[...].astype(jnp.bfloat16), out_ref)
    for i in range(half):
        column = (scal[COL] + i) & 3
        piece = keep(relay_ref[i], scal[FAR + i])
        out_ref[column, 1] = piece
        out_ref[column + half, 1] = piece


def coef_kernel(scal, v_ref, near_far_ref, last_far_ref, x_ref, out_ref):
    half = v_ref.shape[0] // 2
    odd = scal[ODD]
    far_refs = (near_far_ref, last_far_ref)
    x_far = side_of(x_ref, odd)
    far_turn = turn_bf(x_far)
    own_coefs(scal, v_ref, side_of(x_ref, 1 - odd), out_ref)
    for i in range(half):
        column = (scal[COL] + i) & 3
        piece = dot(far_factor(far_refs, i, 0), x_far) + dot(far_factor(far_refs, i, 1), far_turn)
        piece = keep(piece, scal[FAR + i])
        out_ref[column, 1] = piece
        out_ref[column + half, 1] = piece


def resid_kernel(scal, got_ref, u_ref, data_ref, *rest):
    out_ref = rest[-1]
    slots = u_ref.shape[0]
    half = slots // 2
    col, odd = scal[COL], scal[ODD]
    real = jnp.zeros(data_ref.shape, jnp.float32)
    imag = jnp.zeros(data_ref.shape, jnp.float32)
    for s in range(slots):
        column = (col + slots - s) & 3
        way = (col + slots - s) >> 2
        near = jnp.where(odd == 1, way == 0, way == 2)
        relay = jnp.logical_not(jnp.logical_or(near, way == 1)).astype(jnp.int32)
        piece = got_ref[column + half * jnp.where(near, 1 - odd, odd), relay]
        real += left_dot(u_ref[s, 0], piece)
        imag += left_dot(u_ref[s, 1], piece)
    image = real + turn(imag)
    resid = (image - data_ref[...].astype(jnp.float32)).astype(jnp.bfloat16)
    resid_turn = turn_bf(resid)
    for s in range(slots):
        column = (col + slots - s) & 3
        same = ((col + slots - s) >> 2) == 1
        piece = keep(dot(u_ref[s, 0], resid) - dot(u_ref[s, 1], resid_turn), scal[ROW + s])
        place = column + half * jnp.where(same, odd, 1 - odd)
        out_ref[place, 0] = piece
        out_ref[(place + half) & (slots - 1), 1] = piece


def grad_kernel(
    scal, size_ref, got_ref, v_ref, near_far_ref, last_far_ref, x_ref, out_ref, *, first
):
    far_refs = (near_far_ref, last_far_ref)
    slots, _, levels, _ = v_ref.shape
    half = slots // 2
    col, odd = scal[COL], scal[ODD]
    parts, _, part, width = out_ref.shape
    shape = (parts * part, width)
    real = jnp.zeros(shape, jnp.float32)
    imag = jnp.zeros(shape, jnp.float32)
    for s in range(slots):
        column, same, near = outward(col, s, odd)
        piece = got_ref[column + half * jnp.where(same, odd, 1 - odd), 0]
        piece = keep(piece, jnp.where(jnp.logical_or(same, near), levels, 0))
        real += left_dot(v_ref[s, 0], piece)
        imag += left_dot(v_ref[s, 1], piece)
    far_real = jnp.zeros(shape, jnp.float32)
    far_imag = jnp.zeros(shape, jnp.float32)
    for i in range(half):
        column = (col + i) & 3
        valid = (col + i < half).astype(jnp.int32) == odd
        piece = keep(got_ref[column + half * odd, 1], jnp.where(valid, levels, 0))
        far_real += left_dot(far_factor(far_refs, i, 0), piece)
        far_imag += left_dot(far_factor(far_refs, i, 1), piece)
    x = x_ref[...] if first else side_of(x_ref, 1 - odd).astype(jnp.float32)
    size = size_ref[0]
    mine = (x - size * (real - turn(imag))).astype(jnp.bfloat16)
    theirs = (-size * (far_real - turn(far_imag))).astype(jnp.bfloat16)
    for j in range(parts):
        out_ref[j, 1 - odd] = mine[j * part : (j + 1) * part]
        out_ref[j, odd] = theirs[j * part : (j + 1) * part]


def mix_kernel(re_ref, im_ref, got_ref, out_ref):
    count = got_ref.shape[0]
    z, z_turn = [], []
    for g in range(count):
        total = got_ref[g, 0].astype(jnp.float32) + got_ref[g, 1].astype(jnp.float32)
        z.append(total)
        z_turn.append(turn(total))
    for f in range(count):
        total = jnp.zeros_like(z[0])
        for g in range(count):
            total += re_ref[f, g : g + 1, :] * z[g] + im_ref[f, g : g + 1, :] * z_turn[g]
        total = total.astype(jnp.bfloat16)
        for side in range(out_ref.shape[1]):
            out_ref[f, side] = total


def kernel_call(body, shape, scalars, *operands):
    smem = pl.BlockSpec(memory_space=pltpu.SMEM)
    vmem = pl.BlockSpec(memory_space=pltpu.VMEM)
    return pl.pallas_call(
        body,
        out_shape=jax.ShapeDtypeStruct(shape, jnp.bfloat16),
        in_specs=[smem] * len(scalars) + [vmem] * len(operands),
        out_specs=vmem,
        compiler_params=pltpu.CompilerParams(vmem_limit_bytes=VMEM_BYTES),
    )(*scalars, *operands)


def on_device(model_start, data, col_factors, row_factors, ranks, gate_window, step_sizes):
    ntile = lax.axis_size("tile")
    nfreq = lax.axis_size("freq")
    myself = lax.axis_index("tile")
    slots = ranks.shape[2]
    levels = col_factors.shape[3]
    half = slots // 2
    rows_z = ntile // WIDE
    col = myself % WIDE
    odd = (myself // WIDE) % 2
    groups = [[slots * k + i for i in range(slots)] for k in range(ntile // slots)]
    swaps = [
        (z * WIDE + y, (z + 1 if z % 2 else z - 1) * WIDE + y)
        for z in range(1, rows_z - 1)
        for y in range(WIDE)
    ]
    pairs = [
        [
            f * ntile + (z % rows_z) * WIDE + y
            for f in range(nfreq)
            for z in (2 * k - 1, 2 * k)
        ]
        for k in range(rows_z // 2)
        for y in range(WIDE)
    ]

    def spread(pieces):
        return lax.all_to_all(pieces, "tile", 0, 0, tiled=True, axis_index_groups=groups)

    def among_pair(pieces):
        flat = pieces.reshape(2 * nfreq, -1, pieces.shape[-1])
        got = lax.all_to_all(
            flat, ("freq", "tile"), 0, 0, tiled=True, axis_index_groups=pairs
        )
        return got.reshape(pieces.shape)

    model = model_start[0]
    rows, width = model.shape
    part = rows // nfreq
    v, u, observed = col_factors[0], row_factors[0], data[0]

    where = jnp.stack([col, odd])
    vmem = pl.BlockSpec(memory_space=pltpu.VMEM)
    hbm = pl.BlockSpec(memory_space=pltpu.HBM)
    relay, *fars = pl.pallas_call(
        beyond_kernel,
        out_shape=[
            jax.ShapeDtypeStruct(shape, jnp.bfloat16)
            for shape in [(half, levels, width)] + [(half // 2, 2, levels, rows)] * 2
        ],
        in_specs=[pl.BlockSpec(memory_space=pltpu.SMEM), hbm, hbm],
        out_specs=[vmem] * 3,
        scratch_shapes=[
            pltpu.VMEM((rows, width), jnp.float32),
            pltpu.SemaphoreType.DMA((half + 1,)),
        ],
        compiler_params=pltpu.CompilerParams(vmem_limit_bytes=FIRST_VMEM_BYTES),
    )(where, v, model)
    relay = lax.ppermute(relay, "tile", swaps)
    fars = [lax.ppermute(far, "tile", swaps) for far in fars]

    table = ranks[0]
    slot_ids = jnp.arange(slots, dtype=jnp.int32)
    opposite = jnp.clip(myself + jnp.where(odd == 1, WIDE, -WIDE), 0, ntile - 1)
    far_ranks = lax.dynamic_slice(table, (opposite, half * (1 - odd)), (1, half))[0]
    own_ranks = lax.dynamic_index_in_dim(table, myself, 0, keepdims=False)
    anchors = jnp.clip(myself + half - slot_ids, 0, ntile - 1)
    holder = jnp.arange(ntile, dtype=jnp.int32)[:, None] == anchors[None, :]
    row_ranks = jnp.sum(jnp.where(holder, table, 0), axis=0)
    scal = jnp.concatenate([where, own_ranks, far_ranks, row_ranks])
    scal = jnp.pad(scal, (0, SCALARS - scal.shape[0]))

    gate_re, gate_im = gate_matrix(gate_window, nfreq)
    gate_re = jnp.concatenate([gate_re, gate_re], axis=-1)
    gate_im = jnp.concatenate([gate_im, gate_im], axis=-1)

    relay, scal, gate_re, gate_im = lax.optimization_barrier((relay, scal, gate_re, gate_im))
    tiles = (slots, 2, levels, width)
    for step in range(ITERS):
        first = step == 0
        if first:
            coef = kernel_call(first_coef_kernel, tiles, [scal], v, model, relay)
            back = kernel_call(resid_kernel, tiles, [scal], spread(coef), u, observed, fars[0])
        else:
            coef = kernel_call(coef_kernel, tiles, [scal], v, *fars, model)
            back = kernel_call(resid_kernel, tiles, [scal], spread(coef), u, observed)
        z = kernel_call(
            functools.partial(grad_kernel, first=first),
            (nfreq, 2, part, width),
            [scal, step_sizes],
            spread(back),
            v,
            *fars,
            model,
        )
        z = among_pair(z)
        if step == ITERS - 1:
            mixed = kernel_call(mix_kernel, (nfreq, 1, part, width), [], gate_re, gate_im, z)
            model = lax.all_to_all(mixed[:, 0], "freq", 0, 0, tiled=True)
        else:
            mixed = kernel_call(mix_kernel, z.shape, [], gate_re, gate_im, z)
            model = among_pair(mixed)
    return model.reshape(1, rows, width).astype(jnp.float32)


def solution(mesh):
    return jax.shard_map(
        on_device,
        mesh=mesh,
        in_specs=(
            P("freq", "tile", None),
            P("freq", "tile", None),
            P("freq", "tile", None, None, None),
            P("freq", "tile", None, None, None),
            P("freq", None, None),
            P(),
            P("freq"),
        ),
        out_specs=P("freq", "tile", None),
        check_vma=False,
    )
```

```python
import functools
import math

import jax
import jax.numpy as jnp
from jax import lax
from jax.experimental import pallas as pl
from jax.experimental.pallas import tpu as pltpu
from jax.sharding import PartitionSpec as P

NT = 2048
ITERS = 2
WIDE = 4
VMEM_BYTES = 24 * 2**20
FIRST_VMEM_BYTES = 62 * 2**20
COL, ODD, SEAT, INNER, OWN, FAR, ROW, SCALARS = 0, 1, 2, 3, 4, 12, 16, 24


def gate_matrix(window, count):
    start = window[:, 0].astype(jnp.float32)
    span = (window[:, 1] - window[:, 0]).astype(jnp.float32)
    freqs = jnp.arange(count, dtype=jnp.float32)
    delta = freqs[:, None] - freqs[None, :]
    theta = 2.0 * math.pi * delta / NT
    safe = jnp.where(delta == 0.0, 1.0, jnp.sin(theta / 2.0))
    magnitude = jnp.where(
        (delta == 0.0)[:, :, None],
        span[None, None, :] / NT,
        jnp.sin(theta[:, :, None] * span[None, None, :] / 2.0) / (NT * safe[:, :, None]),
    )
    phase = theta[:, :, None] * (start[None, None, :] + (span[None, None, :] - 1.0) / 2.0)
    return (magnitude * jnp.cos(phase), magnitude * jnp.sin(phase))


def turn(z):
    width = z.shape[-1]
    lane = lax.broadcasted_iota(jnp.int32, z.shape, z.ndim - 1)
    rolled = pltpu.roll(z, width // 2, z.ndim - 1)
    return jnp.where(lane < width // 2, -rolled, rolled)


def turn_bf(z):
    return turn(z.astype(jnp.float32)).astype(jnp.bfloat16)


def dot(a, b):
    return jnp.dot(a, b, preferred_element_type=jnp.float32)


def left_dot(a, b):
    return lax.dot_general(a, b, (((0,), (0,)), ((), ())), preferred_element_type=jnp.float32)


def keep(value, rank):
    row = lax.broadcasted_iota(jnp.int32, value.shape, 0)
    return jnp.where(row < rank, value.astype(jnp.float32), 0.0).astype(jnp.bfloat16)


def side_of(ref, side):
    return jnp.concatenate([ref[j, side] for j in range(ref.shape[0])], axis=0)


def far_factor(far_refs, index, which):
    each = far_refs[0].shape[0]
    return far_refs[index // each][index % each, which]


def outward(col, s, odd):
    column = (col + s) & 3
    way = (col + s) >> 2
    same = way == 1
    near = jnp.where(odd == 1, way == 0, way == 2)
    return column, same, near


def beyond_kernel(v_ref, x_ref, out_ref, v_here, x_here, arrived):
    half = out_ref.shape[0]
    odd = 1 - (lax.axis_index("tile") // WIDE) % 2
    copies = [pltpu.make_async_copy(x_ref, x_here, arrived.at[half])]
    for i in range(half):
        tile = v_ref.at[half * odd + i]
        copies.append(pltpu.make_async_copy(tile, v_here.at[i], arrived.at[i]))
    for copy in copies:
        copy.start()
    copies[0].wait()
    x = x_here[...].astype(jnp.bfloat16)
    x_turn = turn_bf(x)
    for i in range(half):
        copies[1 + i].wait()
        piece = dot(v_here[i, 0], x) + dot(v_here[i, 1], x_turn)
        out_ref[i] = piece.astype(jnp.bfloat16)


def own_coefs(scal, v_ref, x, out_ref):
    slots = v_ref.shape[0]
    half = slots // 2
    col, odd, seat = scal[COL], scal[ODD], scal[SEAT]
    x_turn = turn_bf(x)
    for s in range(slots):
        column, same, _ = outward(col, s, odd)
        place = column + half * jnp.where(same, seat, 1 - seat)
        out_ref[place, 0] = keep(dot(v_ref[s, 0], x) + dot(v_ref[s, 1], x_turn), scal[OWN + s])


def first_coef_kernel(scal, v_ref, x_ref, relay_ref, out_ref):
    half = relay_ref.shape[0]
    own_coefs(scal, v_ref, x_ref[...].astype(jnp.bfloat16), out_ref)
    for i in range(half):
        column = (scal[COL] + i) & 3
        piece = keep(relay_ref[i], scal[FAR + i])
        out_ref[column, 1] = piece
        out_ref[column + half, 1] = piece


def coef_kernel(scal, v_ref, near_far_ref, last_far_ref, x_ref, out_ref):
    half = v_ref.shape[0] // 2
    odd = scal[ODD]
    far_refs = (near_far_ref, last_far_ref)
    x_far = side_of(x_ref, odd)
    far_turn = turn_bf(x_far)
    own_coefs(scal, v_ref, side_of(x_ref, 1 - odd), out_ref)
    for i in range(half):
        column = (scal[COL] + i) & 3
        piece = dot(far_factor(far_refs, i, 0), x_far) + dot(far_factor(far_refs, i, 1), far_turn)
        piece = keep(piece, scal[FAR + i])
        out_ref[column, 1] = piece
        out_ref[column + half, 1] = piece


def resid_kernel(scal, got_ref, u_ref, data_ref, *rest):
    out_ref = rest[-1]
    slots = u_ref.shape[0]
    half = slots // 2
    col, odd, seat = scal[COL], scal[ODD], scal[SEAT]
    real = jnp.zeros(data_ref.shape, jnp.float32)
    imag = jnp.zeros(data_ref.shape, jnp.float32)
    for s in range(slots):
        column = (col + slots - s) & 3
        way = (col + slots - s) >> 2
        near = jnp.where(odd == 1, way == 0, way == 2)
        relay = jnp.logical_not(jnp.logical_or(near, way == 1)).astype(jnp.int32)
        piece = got_ref[column + half * jnp.where(near, 1 - seat, seat), relay]
        real += left_dot(u_ref[s, 0], piece)
        imag += left_dot(u_ref[s, 1], piece)
    image = real + turn(imag)
    resid = (image - data_ref[...].astype(jnp.float32)).astype(jnp.bfloat16)
    resid_turn = turn_bf(resid)
    for s in range(slots):
        column = (col + slots - s) & 3
        same = ((col + slots - s) >> 2) == 1
        piece = keep(dot(u_ref[s, 0], resid) - dot(u_ref[s, 1], resid_turn), scal[ROW + s])
        place = column + half * jnp.where(same, seat, 1 - seat)
        out_ref[place, 0] = piece
        out_ref[(place + half) & (slots - 1), 1] = piece


def grad_kernel(
    scal, size_ref, got_ref, v_ref, near_far_ref, last_far_ref, x_ref, out_ref, *, first
):
    far_refs = (near_far_ref, last_far_ref)
    slots, _, levels, _ = v_ref.shape
    half = slots // 2
    col, odd, seat = scal[COL], scal[ODD], scal[SEAT]
    parts, _, part, width = out_ref.shape
    shape = (parts * part, width)
    real = jnp.zeros(shape, jnp.float32)
    imag = jnp.zeros(shape, jnp.float32)
    for s in range(slots):
        column, same, near = outward(col, s, odd)
        piece = got_ref[column + half * jnp.where(same, seat, 1 - seat), 0]
        near = jnp.logical_and(near, scal[INNER] == 1)
        piece = keep(piece, jnp.where(jnp.logical_or(same, near), levels, 0))
        real += left_dot(v_ref[s, 0], piece)
        imag += left_dot(v_ref[s, 1], piece)
    far_real = jnp.zeros(shape, jnp.float32)
    far_imag = jnp.zeros(shape, jnp.float32)
    for i in range(half):
        column = (col + i) & 3
        valid = (col + i < half).astype(jnp.int32) == odd
        piece = keep(got_ref[column + half * seat, 1], jnp.where(valid, levels, 0))
        far_real += left_dot(far_factor(far_refs, i, 0), piece)
        far_imag += left_dot(far_factor(far_refs, i, 1), piece)
    x = x_ref[...] if first else side_of(x_ref, 1 - odd).astype(jnp.float32)
    size = size_ref[0]
    mine = (x - size * (real - turn(imag))).astype(jnp.bfloat16)
    theirs = (-size * (far_real - turn(far_imag))).astype(jnp.bfloat16)
    for j in range(parts):
        out_ref[j, 1 - odd] = mine[j * part : (j + 1) * part]
        out_ref[j, odd] = theirs[j * part : (j + 1) * part]


def mix_kernel(re_ref, im_ref, got_ref, out_ref):
    count = got_ref.shape[0]
    z, z_turn = [], []
    for g in range(count):
        total = got_ref[g, 0].astype(jnp.float32) + got_ref[g, 1].astype(jnp.float32)
        z.append(total)
        z_turn.append(turn(total))
    for f in range(count):
        total = jnp.zeros_like(z[0])
        for g in range(count):
            total += re_ref[f, g : g + 1, :] * z[g] + im_ref[f, g : g + 1, :] * z_turn[g]
        total = total.astype(jnp.bfloat16)
        for side in range(out_ref.shape[1]):
            out_ref[f, side] = total


def kernel_call(body, shape, scalars, *operands):
    smem = pl.BlockSpec(memory_space=pltpu.SMEM)
    vmem = pl.BlockSpec(memory_space=pltpu.VMEM)
    return pl.pallas_call(
        body,
        out_shape=jax.ShapeDtypeStruct(shape, jnp.bfloat16),
        in_specs=[smem] * len(scalars) + [vmem] * len(operands),
        out_specs=vmem,
        compiler_params=pltpu.CompilerParams(vmem_limit_bytes=VMEM_BYTES),
    )(*scalars, *operands)


def on_device(model_start, data, col_factors, row_factors, ranks, gate_window, step_sizes):
    ntile = lax.axis_size("tile")
    nfreq = lax.axis_size("freq")
    myself = lax.axis_index("tile")
    slots = ranks.shape[2]
    levels = col_factors.shape[3]
    half = slots // 2
    rows_z = ntile // WIDE
    col = myself % WIDE
    odd = 1 - (myself // WIDE) % 2
    inner = [
        [f * ntile + slots * k - WIDE + i for i in range(slots)]
        for f in range(nfreq)
        for k in range(1, rows_z // 2)
    ]
    outer = [
        [(f + j) * ntile + z * WIDE + y for j in range(2) for y in range(WIDE)]
        for f in range(0, nfreq, 2)
        for z in (0, rows_z - 1)
    ]
    edge = jnp.logical_or(myself < WIDE, myself >= ntile - WIDE)
    seat = jnp.where(edge, lax.axis_index("freq") % 2, odd)
    swaps = [
        (z * WIDE + y, (z - 1 if z % 2 else z + 1) * WIDE + y)
        for z in range(rows_z)
        for y in range(WIDE)
    ]
    pairs = [
        [
            f * ntile + z * WIDE + y
            for f in range(nfreq)
            for z in (2 * k, 2 * k + 1)
        ]
        for k in range(rows_z // 2)
        for y in range(WIDE)
    ]

    def spread(pieces):
        return lax.all_to_all(
            pieces, ("freq", "tile"), 0, 0, tiled=True, axis_index_groups=inner + outer
        )

    def among_pair(pieces):
        flat = pieces.reshape(2 * nfreq, -1, pieces.shape[-1])
        got = lax.all_to_all(
            flat, ("freq", "tile"), 0, 0, tiled=True, axis_index_groups=pairs
        )
        return got.reshape(pieces.shape)

    model = model_start[0]
    rows, width = model.shape
    part = rows // nfreq
    v, u, observed = col_factors[0], row_factors[0], data[0]

    where = jnp.stack([col, odd, seat, 1 - edge.astype(jnp.int32)])
    hbm = pl.BlockSpec(memory_space=pltpu.HBM)
    relay = pl.pallas_call(
        beyond_kernel,
        out_shape=jax.ShapeDtypeStruct((half, levels, width), jnp.bfloat16),
        in_specs=[hbm, hbm],
        out_specs=pl.BlockSpec(memory_space=pltpu.VMEM),
        scratch_shapes=[
            pltpu.VMEM((half, 2, levels, rows), jnp.bfloat16),
            pltpu.VMEM((rows, width), jnp.float32),
            pltpu.SemaphoreType.DMA((half + 1,)),
        ],
        compiler_params=pltpu.CompilerParams(vmem_limit_bytes=FIRST_VMEM_BYTES),
    )(v, model)
    relay = lax.ppermute(relay, "tile", swaps)
    fars = [
        lax.dynamic_slice_in_dim(v, half * odd + i, half // 2, 0) for i in (0, half // 2)
    ]

    table = ranks[0]
    slot_ids = jnp.arange(slots, dtype=jnp.int32)
    opposite = jnp.clip(myself + jnp.where(odd == 1, WIDE, -WIDE), 0, ntile - 1)
    far_ranks = lax.dynamic_slice(table, (opposite, half * (1 - odd)), (1, half))[0]
    own_ranks = lax.dynamic_index_in_dim(table, myself, 0, keepdims=False)
    receivers = myself + slot_ids - half
    outside = (col + slot_ids) // WIDE == 2 * odd
    exists = (receivers >= 0) & (receivers < ntile)
    own_ranks = jnp.where(exists & jnp.logical_not(outside), own_ranks, 0)
    anchors = myself + half - slot_ids
    holder = jnp.arange(ntile, dtype=jnp.int32)[:, None] == anchors[None, :]
    row_ranks = jnp.sum(jnp.where(holder, table, 0), axis=0)
    scal = jnp.concatenate([where, own_ranks, far_ranks, row_ranks])
    scal = jnp.pad(scal, (0, SCALARS - scal.shape[0]))

    gate_re, gate_im = gate_matrix(gate_window, nfreq)
    gate_re = jnp.concatenate([gate_re, gate_re], axis=-1)
    gate_im = jnp.concatenate([gate_im, gate_im], axis=-1)

    relay, fars, scal, gate_re, gate_im = lax.optimization_barrier(
        (relay, fars, scal, gate_re, gate_im)
    )
    fars = [lax.ppermute(far, "tile", swaps) for far in fars]
    tiles = (slots, 2, levels, width)
    for step in range(ITERS):
        first = step == 0
        if first:
            coef = kernel_call(first_coef_kernel, tiles, [scal], v, model, relay)
            back = kernel_call(resid_kernel, tiles, [scal], spread(coef), u, observed, fars[0])
        else:
            coef = kernel_call(coef_kernel, tiles, [scal], v, *fars, model)
            back = kernel_call(resid_kernel, tiles, [scal], spread(coef), u, observed)
        z = kernel_call(
            functools.partial(grad_kernel, first=first),
            (nfreq, 2, part, width),
            [scal, step_sizes],
            spread(back),
            v,
            *fars,
            model,
        )
        z = among_pair(z)
        if step == ITERS - 1:
            mixed = kernel_call(mix_kernel, (nfreq, 1, part, width), [], gate_re, gate_im, z)
            model = lax.all_to_all(mixed[:, 0], "freq", 0, 0, tiled=True)
        else:
            mixed = kernel_call(mix_kernel, z.shape, [], gate_re, gate_im, z)
            model = among_pair(mixed)
    return model.reshape(1, rows, width).astype(jnp.float32)


def solution(mesh):
    return jax.shard_map(
        on_device,
        mesh=mesh,
        in_specs=(
            P("freq", "tile", None),
            P("freq", "tile", None),
            P("freq", "tile", None, None, None),
            P("freq", "tile", None, None, None),
            P("freq", None, None),
            P(),
            P("freq"),
        ),
        out_specs=P("freq", "tile", None),
        check_vma=False,
    )
```

```python
import functools
import math

import jax
import jax.numpy as jnp
from jax import lax
from jax.experimental import pallas as pl
from jax.experimental.pallas import tpu as pltpu
from jax.sharding import PartitionSpec as P

NT = 2048
ITERS = 2
WIDE = 4
VMEM_BYTES = 24 * 2**20
FIRST_VMEM_BYTES = 215 * 2**18
COL, ODD, SEAT, INNER, OWN, FAR, ROW, SCALARS = 0, 1, 2, 3, 4, 12, 16, 24


def gate_matrix(window, count):
    start = window[:, 0].astype(jnp.float32)
    span = (window[:, 1] - window[:, 0]).astype(jnp.float32)
    freqs = jnp.arange(count, dtype=jnp.float32)
    delta = freqs[:, None] - freqs[None, :]
    theta = 2.0 * math.pi * delta / NT
    safe = jnp.where(delta == 0.0, 1.0, jnp.sin(theta / 2.0))
    magnitude = jnp.where(
        (delta == 0.0)[:, :, None],
        span[None, None, :] / NT,
        jnp.sin(theta[:, :, None] * span[None, None, :] / 2.0) / (NT * safe[:, :, None]),
    )
    phase = theta[:, :, None] * (start[None, None, :] + (span[None, None, :] - 1.0) / 2.0)
    return (magnitude * jnp.cos(phase), magnitude * jnp.sin(phase))


def turn(z):
    width = z.shape[-1]
    lane = lax.broadcasted_iota(jnp.int32, z.shape, z.ndim - 1)
    rolled = pltpu.roll(z, width // 2, z.ndim - 1)
    return jnp.where(lane < width // 2, -rolled, rolled)


def turn_bf(z):
    return turn(z.astype(jnp.float32)).astype(jnp.bfloat16)


def dot(a, b):
    return jnp.dot(a, b, preferred_element_type=jnp.float32)


def left_dot(a, b):
    return lax.dot_general(a, b, (((0,), (0,)), ((), ())), preferred_element_type=jnp.float32)


def stacked(ref, which):
    return jnp.concatenate([ref[s, which] for s in range(ref.shape[0])], axis=0)


def keep(value, rank):
    row = lax.broadcasted_iota(jnp.int32, value.shape, 0)
    return jnp.where(row < rank, value.astype(jnp.float32), 0.0).astype(jnp.bfloat16)


def side_of(ref, side):
    return jnp.concatenate([ref[j, side] for j in range(ref.shape[0])], axis=0)


def far_factor(far_refs, index, which):
    each = far_refs[0].shape[0]
    return far_refs[index // each][index % each, which]


def outward(col, s, odd):
    column = (col + s) & 3
    way = (col + s) >> 2
    same = way == 1
    near = jnp.where(odd == 1, way == 0, way == 2)
    return column, same, near


def beyond_kernel(v_ref, x_ref, out_ref, v_here, x_here, arrived):
    half = out_ref.shape[0]
    odd = 1 - (lax.axis_index("tile") // WIDE) % 2
    copies = [pltpu.make_async_copy(x_ref, x_here, arrived.at[half])]
    for i in range(half):
        tile = v_ref.at[half * odd + i]
        copies.append(pltpu.make_async_copy(tile, v_here.at[i], arrived.at[i]))
    for copy in copies:
        copy.start()
    copies[0].wait()
    x = x_here[...].astype(jnp.bfloat16)
    x_turn = turn_bf(x)
    for i in range(half):
        copies[1 + i].wait()
        piece = dot(v_here[i, 0], x) + dot(v_here[i, 1], x_turn)
        out_ref[i] = piece.astype(jnp.bfloat16)


def own_coefs(scal, v_ref, x, out_ref):
    slots = v_ref.shape[0]
    half = slots // 2
    col, odd, seat = scal[COL], scal[ODD], scal[SEAT]
    x_turn = turn_bf(x)
    for s in range(slots):
        column, same, _ = outward(col, s, odd)
        place = column + half * jnp.where(same, seat, 1 - seat)
        out_ref[place, 0] = keep(dot(v_ref[s, 0], x) + dot(v_ref[s, 1], x_turn), scal[OWN + s])


def first_coef_kernel(scal, v_ref, x_ref, relay_ref, out_ref):
    half = relay_ref.shape[0]
    own_coefs(scal, v_ref, x_ref[...].astype(jnp.bfloat16), out_ref)
    for i in range(half):
        column = (scal[COL] + i) & 3
        piece = keep(relay_ref[i], scal[FAR + i])
        out_ref[column, 1] = piece
        out_ref[column + half, 1] = piece


def coef_kernel(scal, v_ref, near_far_ref, last_far_ref, x_ref, out_ref):
    half = v_ref.shape[0] // 2
    odd = scal[ODD]
    far_refs = (near_far_ref, last_far_ref)
    x_far = side_of(x_ref, odd)
    far_turn = turn_bf(x_far)
    own_coefs(scal, v_ref, side_of(x_ref, 1 - odd), out_ref)
    for i in range(half):
        column = (scal[COL] + i) & 3
        piece = dot(far_factor(far_refs, i, 0), x_far) + dot(far_factor(far_refs, i, 1), far_turn)
        piece = keep(piece, scal[FAR + i])
        out_ref[column, 1] = piece
        out_ref[column + half, 1] = piece


def resid_kernel(scal, got_ref, u_ref, data_ref, *rest):
    out_ref, placed = rest[-2:]
    slots = u_ref.shape[0]
    half = slots // 2
    col, odd, seat = scal[COL], scal[ODD], scal[SEAT]
    for s in range(slots):
        column = (col + slots - s) & 3
        way = (col + slots - s) >> 2
        near = jnp.where(odd == 1, way == 0, way == 2)
        relay = jnp.logical_not(jnp.logical_or(near, way == 1)).astype(jnp.int32)
        placed[s] = got_ref[column + half * jnp.where(near, 1 - seat, seat), relay]
    values = placed[...].reshape(-1, placed.shape[-1])
    image = left_dot(stacked(u_ref, 0), values) + turn(left_dot(stacked(u_ref, 1), values))
    resid = (image - data_ref[...].astype(jnp.float32)).astype(jnp.bfloat16)
    resid_turn = turn_bf(resid)
    for s in range(slots):
        column = (col + slots - s) & 3
        same = ((col + slots - s) >> 2) == 1
        piece = keep(dot(u_ref[s, 0], resid) - dot(u_ref[s, 1], resid_turn), scal[ROW + s])
        place = column + half * jnp.where(same, seat, 1 - seat)
        out_ref[place, 0] = piece
        out_ref[(place + half) & (slots - 1), 1] = piece


def grad_kernel(
    scal, size_ref, got_ref, v_ref, near_far_ref, last_far_ref, x_ref, out_ref, landed, *, first
):
    far_refs = (near_far_ref, last_far_ref)
    slots, _, levels, _ = v_ref.shape
    half = slots // 2
    col, odd, seat = scal[COL], scal[ODD], scal[SEAT]
    parts, _, part, width = out_ref.shape
    shape = (parts * part, width)
    for s in range(slots):
        column, same, near = outward(col, s, odd)
        piece = got_ref[column + half * jnp.where(same, seat, 1 - seat), 0]
        near = jnp.logical_and(near, scal[INNER] == 1)
        landed[s] = keep(piece, jnp.where(jnp.logical_or(same, near), levels, 0))
    values = landed[...].reshape(-1, width)
    real = left_dot(stacked(v_ref, 0), values)
    imag = left_dot(stacked(v_ref, 1), values)
    far_real = jnp.zeros(shape, jnp.float32)
    far_imag = jnp.zeros(shape, jnp.float32)
    for i in range(half):
        column = (col + i) & 3
        valid = (col + i < half).astype(jnp.int32) == odd
        piece = keep(got_ref[column + half * seat, 1], jnp.where(valid, levels, 0))
        far_real += left_dot(far_factor(far_refs, i, 0), piece)
        far_imag += left_dot(far_factor(far_refs, i, 1), piece)
    x = x_ref[...] if first else side_of(x_ref, 1 - odd).astype(jnp.float32)
    size = size_ref[0]
    mine = (x - size * (real - turn(imag))).astype(jnp.bfloat16)
    theirs = (-size * (far_real - turn(far_imag))).astype(jnp.bfloat16)
    for j in range(parts):
        out_ref[j, 1 - odd] = mine[j * part : (j + 1) * part]
        out_ref[j, odd] = theirs[j * part : (j + 1) * part]


def mix_kernel(re_ref, im_ref, got_ref, out_ref):
    count = got_ref.shape[0]
    z, z_turn = [], []
    for g in range(count):
        total = got_ref[g, 0].astype(jnp.float32) + got_ref[g, 1].astype(jnp.float32)
        z.append(total)
        z_turn.append(turn(total))
    for f in range(count):
        total = jnp.zeros_like(z[0])
        for g in range(count):
            total += re_ref[f, g : g + 1, :] * z[g] + im_ref[f, g : g + 1, :] * z_turn[g]
        total = total.astype(jnp.bfloat16)
        for side in range(out_ref.shape[1]):
            out_ref[f, side] = total


def kernel_call(body, shape, scalars, *operands, scratch=()):
    smem = pl.BlockSpec(memory_space=pltpu.SMEM)
    vmem = pl.BlockSpec(memory_space=pltpu.VMEM)
    return pl.pallas_call(
        body,
        out_shape=jax.ShapeDtypeStruct(shape, jnp.bfloat16),
        in_specs=[smem] * len(scalars) + [vmem] * len(operands),
        out_specs=vmem,
        scratch_shapes=[pltpu.VMEM(held, jnp.bfloat16) for held in scratch],
        compiler_params=pltpu.CompilerParams(vmem_limit_bytes=VMEM_BYTES),
    )(*scalars, *operands)


def on_device(model_start, data, col_factors, row_factors, ranks, gate_window, step_sizes):
    ntile = lax.axis_size("tile")
    nfreq = lax.axis_size("freq")
    myself = lax.axis_index("tile")
    slots = ranks.shape[2]
    levels = col_factors.shape[3]
    half = slots // 2
    rows_z = ntile // WIDE
    col = myself % WIDE
    odd = 1 - (myself // WIDE) % 2
    inner = [
        [f * ntile + slots * k - WIDE + i for i in range(slots)]
        for f in range(nfreq)
        for k in range(1, rows_z // 2)
    ]
    outer = [
        [(f + j) * ntile + z * WIDE + y for j in range(2) for y in range(WIDE)]
        for f in range(0, nfreq, 2)
        for z in (0, rows_z - 1)
    ]
    edge = jnp.logical_or(myself < WIDE, myself >= ntile - WIDE)
    seat = jnp.where(edge, lax.axis_index("freq") % 2, odd)
    swaps = [
        (z * WIDE + y, (z - 1 if z % 2 else z + 1) * WIDE + y)
        for z in range(rows_z)
        for y in range(WIDE)
    ]
    pairs = [
        [
            f * ntile + z * WIDE + y
            for f in range(nfreq)
            for z in (2 * k, 2 * k + 1)
        ]
        for k in range(rows_z // 2)
        for y in range(WIDE)
    ]

    def spread(pieces):
        return lax.all_to_all(
            pieces, ("freq", "tile"), 0, 0, tiled=True, axis_index_groups=inner + outer
        )

    def among_pair(pieces):
        flat = pieces.reshape(2 * nfreq, -1, pieces.shape[-1])
        got = lax.all_to_all(
            flat, ("freq", "tile"), 0, 0, tiled=True, axis_index_groups=pairs
        )
        return got.reshape(pieces.shape)

    model = model_start[0]
    rows, width = model.shape
    part = rows // nfreq
    v, u, observed = col_factors[0], row_factors[0], data[0]

    where = jnp.stack([col, odd, seat, 1 - edge.astype(jnp.int32)])
    hbm = pl.BlockSpec(memory_space=pltpu.HBM)
    relay = pl.pallas_call(
        beyond_kernel,
        out_shape=jax.ShapeDtypeStruct((half, levels, width), jnp.bfloat16),
        in_specs=[hbm, hbm],
        out_specs=pl.BlockSpec(memory_space=pltpu.VMEM),
        scratch_shapes=[
            pltpu.VMEM((half, 2, levels, rows), jnp.bfloat16),
            pltpu.VMEM((rows, width), jnp.float32),
            pltpu.SemaphoreType.DMA((half + 1,)),
        ],
        compiler_params=pltpu.CompilerParams(vmem_limit_bytes=FIRST_VMEM_BYTES),
    )(v, model)
    v, relay = lax.optimization_barrier((v, relay))
    relay = lax.ppermute(relay, "tile", swaps)
    fars = [
        lax.dynamic_slice_in_dim(v, half * odd + i, half // 2, 0) for i in (0, half // 2)
    ]

    table = ranks[0]
    slot_ids = jnp.arange(slots, dtype=jnp.int32)
    opposite = jnp.clip(myself + jnp.where(odd == 1, WIDE, -WIDE), 0, ntile - 1)
    far_ranks = lax.dynamic_slice(table, (opposite, half * (1 - odd)), (1, half))[0]
    own_ranks = lax.dynamic_index_in_dim(table, myself, 0, keepdims=False)
    receivers = myself + slot_ids - half
    outside = (col + slot_ids) // WIDE == 2 * odd
    exists = (receivers >= 0) & (receivers < ntile)
    own_ranks = jnp.where(exists & jnp.logical_not(outside), own_ranks, 0)
    anchors = myself + half - slot_ids
    holder = jnp.arange(ntile, dtype=jnp.int32)[:, None] == anchors[None, :]
    row_ranks = jnp.sum(jnp.where(holder, table, 0), axis=0)
    scal = jnp.concatenate([where, own_ranks, far_ranks, row_ranks])
    scal = jnp.pad(scal, (0, SCALARS - scal.shape[0]))

    gate_re, gate_im = gate_matrix(gate_window, nfreq)
    gate_re = jnp.concatenate([gate_re, gate_re], axis=-1)
    gate_im = jnp.concatenate([gate_im, gate_im], axis=-1)

    relay, fars, scal, gate_re, gate_im = lax.optimization_barrier(
        (relay, fars, scal, gate_re, gate_im)
    )
    fars = [lax.ppermute(far, "tile", swaps) for far in fars]
    tiles = (slots, 2, levels, width)
    pieces = [(slots, levels, width)]
    for step in range(ITERS):
        first = step == 0
        if first:
            coef = kernel_call(first_coef_kernel, tiles, [scal], v, model, relay)
            early = (fars[0],)
        else:
            coef = kernel_call(coef_kernel, tiles, [scal], v, *fars, model)
            early = ()
        back = kernel_call(
            resid_kernel, tiles, [scal], spread(coef), u, observed, *early, scratch=pieces
        )
        z = kernel_call(
            functools.partial(grad_kernel, first=first),
            (nfreq, 2, part, width),
            [scal, step_sizes],
            spread(back),
            v,
            *fars,
            model,
            scratch=pieces,
        )
        z = among_pair(z)
        if step == ITERS - 1:
            mixed = kernel_call(mix_kernel, (nfreq, 1, part, width), [], gate_re, gate_im, z)
            model = lax.all_to_all(mixed[:, 0], "freq", 0, 0, tiled=True)
        else:
            mixed = kernel_call(mix_kernel, z.shape, [], gate_re, gate_im, z)
            model = among_pair(mixed)
    return model.reshape(1, rows, width).astype(jnp.float32)


def solution(mesh):
    return jax.shard_map(
        on_device,
        mesh=mesh,
        in_specs=(
            P("freq", "tile", None),
            P("freq", "tile", None),
            P("freq", "tile", None, None, None),
            P("freq", "tile", None, None, None),
            P("freq", None, None),
            P(),
            P("freq"),
        ),
        out_specs=P("freq", "tile", None),
        check_vma=False,
    )
```

```python
import functools
import math

import jax
import jax.numpy as jnp
from jax import lax
from jax.experimental import pallas as pl
from jax.experimental.pallas import tpu as pltpu
from jax.sharding import PartitionSpec as P

NT = 2048
ITERS = 2
WIDE = 4
VMEM_BYTES = 24 * 2**20
FIRST_VMEM_BYTES = 215 * 2**18
COL, ODD, SEAT, INNER, OWN, FAR, ROW, SCALARS = 0, 1, 2, 3, 4, 12, 16, 24


def gate_matrix(window, count):
    start = window[:, 0].astype(jnp.float32)
    span = (window[:, 1] - window[:, 0]).astype(jnp.float32)
    freqs = jnp.arange(count, dtype=jnp.float32)
    delta = freqs[:, None] - freqs[None, :]
    theta = 2.0 * math.pi * delta / NT
    safe = jnp.where(delta == 0.0, 1.0, jnp.sin(theta / 2.0))
    magnitude = jnp.where(
        (delta == 0.0)[:, :, None],
        span[None, None, :] / NT,
        jnp.sin(theta[:, :, None] * span[None, None, :] / 2.0) / (NT * safe[:, :, None]),
    )
    phase = theta[:, :, None] * (start[None, None, :] + (span[None, None, :] - 1.0) / 2.0)
    return (magnitude * jnp.cos(phase), magnitude * jnp.sin(phase))


def turn(z):
    width = z.shape[-1]
    lane = lax.broadcasted_iota(jnp.int32, z.shape, z.ndim - 1)
    rolled = pltpu.roll(z, width // 2, z.ndim - 1)
    return jnp.where(lane < width // 2, -rolled, rolled)


def turn_bf(z):
    return turn(z.astype(jnp.float32)).astype(jnp.bfloat16)


def dot(a, b):
    return jnp.dot(a, b, preferred_element_type=jnp.float32)


def left_dot(a, b):
    return lax.dot_general(a, b, (((0,), (0,)), ((), ())), preferred_element_type=jnp.float32)


def stacked(ref, which):
    return jnp.concatenate([ref[s, which] for s in range(ref.shape[0])], axis=0)


def keep(value, rank):
    row = lax.broadcasted_iota(jnp.int32, value.shape, 0)
    return jnp.where(row < rank, value.astype(jnp.float32), 0.0).astype(jnp.bfloat16)


def side_of(ref, side):
    return jnp.concatenate([ref[j, side] for j in range(ref.shape[0])], axis=0)


def far_factor(far_refs, index, which):
    each = far_refs[0].shape[0]
    return far_refs[index // each][index % each, which]


def outward(col, s, odd):
    column = (col + s) & 3
    way = (col + s) >> 2
    same = way == 1
    near = jnp.where(odd == 1, way == 0, way == 2)
    return column, same, near


def beyond_kernel(v_ref, x_ref, out_ref, v_here, x_here, arrived):
    half = out_ref.shape[0]
    odd = 1 - (lax.axis_index("tile") // WIDE) % 2
    copies = [pltpu.make_async_copy(x_ref, x_here, arrived.at[half])]
    for i in range(half):
        tile = v_ref.at[half * odd + i]
        copies.append(pltpu.make_async_copy(tile, v_here.at[i], arrived.at[i]))
    for copy in copies:
        copy.start()
    copies[0].wait()
    x = x_here[...].astype(jnp.bfloat16)
    x_turn = turn_bf(x)
    for i in range(half):
        copies[1 + i].wait()
        piece = dot(v_here[i, 0], x) + dot(v_here[i, 1], x_turn)
        out_ref[i] = piece.astype(jnp.bfloat16)


def own_coefs(scal, v_ref, x, out_ref):
    slots = v_ref.shape[0]
    half = slots // 2
    col, odd, seat = scal[COL], scal[ODD], scal[SEAT]
    x_turn = turn_bf(x)
    for s in range(slots):
        column, same, _ = outward(col, s, odd)
        place = column + half * jnp.where(same, seat, 1 - seat)
        out_ref[place, 0] = keep(dot(v_ref[s, 0], x) + dot(v_ref[s, 1], x_turn), scal[OWN + s])


def first_coef_kernel(scal, v_ref, x_ref, relay_ref, out_ref):
    half = relay_ref.shape[0]
    own_coefs(scal, v_ref, x_ref[...].astype(jnp.bfloat16), out_ref)
    for i in range(half):
        column = (scal[COL] + i) & 3
        piece = keep(relay_ref[i], scal[FAR + i])
        out_ref[column, 1] = piece
        out_ref[column + half, 1] = piece


def coef_kernel(scal, v_ref, near_far_ref, last_far_ref, x_ref, out_ref):
    half = v_ref.shape[0] // 2
    odd = scal[ODD]
    far_refs = (near_far_ref, last_far_ref)
    x_far = side_of(x_ref, odd)
    far_turn = turn_bf(x_far)
    own_coefs(scal, v_ref, side_of(x_ref, 1 - odd), out_ref)
    for i in range(half):
        column = (scal[COL] + i) & 3
        piece = dot(far_factor(far_refs, i, 0), x_far) + dot(far_factor(far_refs, i, 1), far_turn)
        piece = keep(piece, scal[FAR + i])
        out_ref[column, 1] = piece
        out_ref[column + half, 1] = piece


def resid_kernel(scal, got_ref, u_ref, data_ref, *rest):
    out_ref, placed = rest[-2:]
    slots = u_ref.shape[0]
    half = slots // 2
    col, odd, seat = scal[COL], scal[ODD], scal[SEAT]
    for s in range(slots):
        column = (col + slots - s) & 3
        way = (col + slots - s) >> 2
        near = jnp.where(odd == 1, way == 0, way == 2)
        relay = jnp.logical_not(jnp.logical_or(near, way == 1)).astype(jnp.int32)
        placed[s] = got_ref[column + half * jnp.where(near, 1 - seat, seat), relay]
    values = placed[...].reshape(-1, placed.shape[-1])
    image = left_dot(stacked(u_ref, 0), values) + turn(left_dot(stacked(u_ref, 1), values))
    resid = (image - data_ref[...].astype(jnp.float32)).astype(jnp.bfloat16)
    resid_turn = turn_bf(resid)
    for s in range(slots):
        column = (col + slots - s) & 3
        same = ((col + slots - s) >> 2) == 1
        piece = keep(dot(u_ref[s, 0], resid) - dot(u_ref[s, 1], resid_turn), scal[ROW + s])
        place = column + half * jnp.where(same, seat, 1 - seat)
        out_ref[place, 0] = piece
        out_ref[(place + half) & (slots - 1), 1] = piece


def grad_kernel(
    scal, size_ref, got_ref, v_ref, near_far_ref, last_far_ref, x_ref, out_ref, landed, *, first
):
    far_refs = (near_far_ref, last_far_ref)
    slots, _, levels, _ = v_ref.shape
    half = slots // 2
    col, odd, seat = scal[COL], scal[ODD], scal[SEAT]
    parts, _, part, width = out_ref.shape
    shape = (parts * part, width)
    for s in range(slots):
        column, same, near = outward(col, s, odd)
        piece = got_ref[column + half * jnp.where(same, seat, 1 - seat), 0]
        near = jnp.logical_and(near, scal[INNER] == 1)
        landed[s] = keep(piece, jnp.where(jnp.logical_or(same, near), levels, 0))
    values = landed[...].reshape(-1, width)
    real = left_dot(stacked(v_ref, 0), values)
    imag = left_dot(stacked(v_ref, 1), values)
    far_real = jnp.zeros(shape, jnp.float32)
    far_imag = jnp.zeros(shape, jnp.float32)
    for i in range(half):
        column = (col + i) & 3
        valid = (col + i < half).astype(jnp.int32) == odd
        piece = keep(got_ref[column + half * seat, 1], jnp.where(valid, levels, 0))
        far_real += left_dot(far_factor(far_refs, i, 0), piece)
        far_imag += left_dot(far_factor(far_refs, i, 1), piece)
    x = x_ref[...] if first else side_of(x_ref, 1 - odd).astype(jnp.float32)
    size = size_ref[0]
    mine = (x - size * (real - turn(imag))).astype(jnp.bfloat16)
    theirs = (-size * (far_real - turn(far_imag))).astype(jnp.bfloat16)
    for j in range(parts):
        out_ref[j, 1 - odd] = mine[j * part : (j + 1) * part]
        out_ref[j, odd] = theirs[j * part : (j + 1) * part]


def mix_kernel(re_ref, im_ref, got_ref, out_ref):
    count = got_ref.shape[0]
    z, z_turn = [], []
    for g in range(count):
        total = got_ref[g, 0].astype(jnp.float32) + got_ref[g, 1].astype(jnp.float32)
        z.append(total)
        z_turn.append(turn(total))
    for f in range(count):
        total = jnp.zeros_like(z[0])
        for g in range(count):
            total += re_ref[f, g : g + 1, :] * z[g] + im_ref[f, g : g + 1, :] * z_turn[g]
        total = total.astype(out_ref.dtype)
        for side in range(out_ref.shape[1]):
            out_ref[f, side] = total


def kernel_call(body, shape, scalars, *operands, scratch=(), dtype=jnp.bfloat16):
    smem = pl.BlockSpec(memory_space=pltpu.SMEM)
    vmem = pl.BlockSpec(memory_space=pltpu.VMEM)
    return pl.pallas_call(
        body,
        out_shape=jax.ShapeDtypeStruct(shape, dtype),
        in_specs=[smem] * len(scalars) + [vmem] * len(operands),
        out_specs=vmem,
        scratch_shapes=[pltpu.VMEM(held, jnp.bfloat16) for held in scratch],
        compiler_params=pltpu.CompilerParams(vmem_limit_bytes=VMEM_BYTES),
    )(*scalars, *operands)


def on_device(model_start, data, col_factors, row_factors, ranks, gate_window, step_sizes):
    ntile = lax.axis_size("tile")
    nfreq = lax.axis_size("freq")
    myself = lax.axis_index("tile")
    slots = ranks.shape[2]
    levels = col_factors.shape[3]
    half = slots // 2
    rows_z = ntile // WIDE
    col = myself % WIDE
    odd = 1 - (myself // WIDE) % 2
    inner = [
        [f * ntile + slots * k - WIDE + i for i in range(slots)]
        for f in range(nfreq)
        for k in range(1, rows_z // 2)
    ]
    outer = [
        [(f + j) * ntile + z * WIDE + y for j in range(2) for y in range(WIDE)]
        for f in range(0, nfreq, 2)
        for z in (0, rows_z - 1)
    ]
    edge = jnp.logical_or(myself < WIDE, myself >= ntile - WIDE)
    seat = jnp.where(edge, lax.axis_index("freq") % 2, odd)
    swaps = [
        (z * WIDE + y, (z - 1 if z % 2 else z + 1) * WIDE + y)
        for z in range(rows_z)
        for y in range(WIDE)
    ]
    pairs = [
        [
            f * ntile + z * WIDE + y
            for f in range(nfreq)
            for z in (2 * k, 2 * k + 1)
        ]
        for k in range(rows_z // 2)
        for y in range(WIDE)
    ]

    def spread(pieces):
        return lax.all_to_all(
            pieces, ("freq", "tile"), 0, 0, tiled=True, axis_index_groups=inner + outer
        )

    def among_pair(pieces):
        flat = pieces.reshape(2 * nfreq, -1, pieces.shape[-1])
        got = lax.all_to_all(
            flat, ("freq", "tile"), 0, 0, tiled=True, axis_index_groups=pairs
        )
        return got.reshape(pieces.shape)

    model = model_start[0]
    rows, width = model.shape
    part = rows // nfreq
    v, u, observed = col_factors[0], row_factors[0], data[0]

    where = jnp.stack([col, odd, seat, 1 - edge.astype(jnp.int32)])
    hbm = pl.BlockSpec(memory_space=pltpu.HBM)
    relay = pl.pallas_call(
        beyond_kernel,
        out_shape=jax.ShapeDtypeStruct((half, levels, width), jnp.bfloat16),
        in_specs=[hbm, hbm],
        out_specs=pl.BlockSpec(memory_space=pltpu.VMEM),
        scratch_shapes=[
            pltpu.VMEM((half, 2, levels, rows), jnp.bfloat16),
            pltpu.VMEM((rows, width), jnp.float32),
            pltpu.SemaphoreType.DMA((half + 1,)),
        ],
        compiler_params=pltpu.CompilerParams(vmem_limit_bytes=FIRST_VMEM_BYTES),
    )(v, model)
    v, relay = lax.optimization_barrier((v, relay))
    relay = lax.ppermute(relay, "tile", swaps)
    fars = [
        lax.dynamic_slice_in_dim(v, half * odd + i, half // 2, 0) for i in (0, half // 2)
    ]

    table = ranks[0]
    slot_ids = jnp.arange(slots, dtype=jnp.int32)
    opposite = jnp.clip(myself + jnp.where(odd == 1, WIDE, -WIDE), 0, ntile - 1)
    far_ranks = lax.dynamic_slice(table, (opposite, half * (1 - odd)), (1, half))[0]
    own_ranks = lax.dynamic_index_in_dim(table, myself, 0, keepdims=False)
    receivers = myself + slot_ids - half
    outside = (col + slot_ids) // WIDE == 2 * odd
    exists = (receivers >= 0) & (receivers < ntile)
    own_ranks = jnp.where(exists & jnp.logical_not(outside), own_ranks, 0)
    anchors = myself + half - slot_ids
    holder = jnp.arange(ntile, dtype=jnp.int32)[:, None] == anchors[None, :]
    row_ranks = jnp.sum(jnp.where(holder, table, 0), axis=0)
    scal = jnp.concatenate([where, own_ranks, far_ranks, row_ranks])
    scal = jnp.pad(scal, (0, SCALARS - scal.shape[0]))

    gate_re, gate_im = gate_matrix(gate_window, nfreq)
    gate_re = jnp.concatenate([gate_re, gate_re], axis=-1)
    gate_im = jnp.concatenate([gate_im, gate_im], axis=-1)

    relay, fars, scal, gate_re, gate_im = lax.optimization_barrier(
        (relay, fars, scal, gate_re, gate_im)
    )
    fars = [lax.ppermute(far, "tile", swaps) for far in fars]
    tiles = (slots, 2, levels, width)
    pieces = [(slots, levels, width)]
    for step in range(ITERS):
        first = step == 0
        if first:
            coef = kernel_call(first_coef_kernel, tiles, [scal], v, model, relay)
            early = (fars[0],)
        else:
            coef = kernel_call(coef_kernel, tiles, [scal], v, *fars, model)
            early = ()
        back = kernel_call(
            resid_kernel, tiles, [scal], spread(coef), u, observed, *early, scratch=pieces
        )
        z = kernel_call(
            functools.partial(grad_kernel, first=first),
            (nfreq, 2, part, width),
            [scal, step_sizes],
            spread(back),
            v,
            *fars,
            model,
            scratch=pieces,
        )
        z = among_pair(z)
        if step == ITERS - 1:
            mixed = kernel_call(
                mix_kernel,
                (nfreq, 1, part, width),
                [],
                gate_re,
                gate_im,
                z,
                dtype=jnp.float32,
            )
            model = lax.all_to_all(mixed[:, 0], "freq", 0, 0, tiled=True)
        else:
            mixed = kernel_call(mix_kernel, z.shape, [], gate_re, gate_im, z)
            model = among_pair(mixed)
    return model.reshape(1, rows, width).astype(jnp.float32)


def solution(mesh):
    return jax.shard_map(
        on_device,
        mesh=mesh,
        in_specs=(
            P("freq", "tile", None),
            P("freq", "tile", None),
            P("freq", "tile", None, None, None),
            P("freq", "tile", None, None, None),
            P("freq", None, None),
            P(),
            P("freq"),
        ),
        out_specs=P("freq", "tile", None),
        check_vma=False,
    )
```
